32 devices in a mesh: hil: 8 (over z, x), vec: 4 (over y, core).
Axes of the slice: x: 2, y: 2, z: 4, core: 2. Of those that a mesh axis runs over, the one named last changes fastest.
Arguments:
- start_block: float32 [1024, 64, 1024], P('hil', 'vec'), may hold values from -10800 to 10800
- down_matrix: float32 [1024, 1024], replicated, may hold values from -1 to 1, as said below
- hop_partner: int32 [10, 1024], replicated, may hold values from 0 to 1023, as said below
- hop_sign: int32 [10, 1024], replicated, may hold values from -1 to 1
- bond_hop: float32 [10], replicated, may hold values from 0.3 to 1
- onsite_u: float32 [10], replicated, may hold values from 0.5 to 2
Outputs:
- filtered_vectors: float32 [1024, 64, 1024], P('hil', 'vec')
The draws below stay inside these ranges and needn't reach their ends.
Inputs may be any that keep to these rules, and one draw needn't show every extreme that they name: down_matrix is symmetric. For every b and u: hop_partner[b, hop_partner[b, u]] = u, hop_sign[b, hop_partner[b, u]] = hop_sign[b, u], and hop_partner[b, u] = u wherever hop_sign[b, u] = 0.
All inputs are finite; a program needn't handle non-finite values.
Results may differ from the reference program's by a relative error of at most 0.0002.
Values sent between devices are 32-bit elements; how exact they have to be, the bound alone decides.
No kernel may reach another device: no remote copies, remote signals or barrier semaphores. Data moves between devices by JAX's collectives and lax.ppermute only.
A program may use at most 192 MiB of HBM per device.

```python
import math
import jax
import jax.numpy as jnp
from jax import lax

SITES = 10
NU = 1024
ND = 1024
NVEC = 64
BONDS = 10
DEGREE = 2
NS_ITERS = 4
OUTER = 1


def draw_start_block(key, part):
    key_values, key_rows, key_cols = jax.random.split(jax.random.fold_in(key, 11), 3)
    row_scale = jnp.exp(jax.random.uniform(key_rows, (NU,), jnp.float32, 0.0, math.log(10.0)))
    col_scale = jnp.exp(jax.random.uniform(key_cols, (NVEC,), jnp.float32, 0.0, math.log(30.0)))
    positions = jnp.arange(NU, dtype=jnp.float32) / NU
    values = jax.random.truncated_normal(key_values, -4.0, 4.0, (NU, NVEC, ND), jnp.float32)
    row_scale = row_scale * jnp.exp(math.log(3.0) * positions)
    return values * row_scale[:, None, None] * col_scale[None, :, None]


def draw_down_matrix(key, part):
    base_key = jax.random.fold_in(key, 23)
    base = jax.random.truncated_normal(base_key, -4.0, 4.0, (ND, ND), jnp.float32)
    return (base + base.T) / math.sqrt(2.0 * ND)


def bond_table(key):
    key_first, key_offset, key_wide = jax.random.split(jax.random.fold_in(key, 37), 3)
    first_site = jax.random.randint(key_first, (BONDS,), 0, SITES)
    offset = jax.random.randint(key_offset, (BONDS,), 1, SITES)
    wide_offset = jax.random.randint(key_wide, (BONDS,), 2, SITES - 1)
    offset = jnp.where(jnp.arange(BONDS) == 0, wide_offset, offset)
    second_site = (first_site + offset) % SITES
    low_site = jnp.minimum(first_site, second_site)[:, None]
    high_site = jnp.maximum(first_site, second_site)[:, None]
    states = jnp.arange(NU, dtype=jnp.int32)
    sites_all = jnp.arange(SITES, dtype=jnp.int32)
    occupied = jnp.bitwise_and(jnp.right_shift(states[None, :], sites_all[:, None]), 1)
    between = jnp.logical_and(sites_all[None, :] > low_site, sites_all[None, :] < high_site).astype(jnp.int32)
    crossed = jnp.sum(between[:, :, None] * occupied[None, :, :], axis=1)
    low_bit = jnp.bitwise_and(jnp.right_shift(states[None, :], low_site), 1)
    high_bit = jnp.bitwise_and(jnp.right_shift(states[None, :], high_site), 1)
    allowed = low_bit != high_bit
    hop_signs = jnp.where(allowed, 1 - 2 * (crossed % 2), 0)
    flip_mask = jnp.left_shift(1, low_site) + jnp.left_shift(1, high_site)
    partner = jnp.where(allowed, jnp.bitwise_xor(states[None, :], flip_mask), states[None, :])
    return (partner.astype(jnp.int32), hop_signs.astype(jnp.int32))


def draw_hop_partner(key, part):
    return bond_table(key)[0]


def draw_hop_sign(key, part):
    return bond_table(key)[1]


def setup_inputs(seed: int = 0) -> dict:
    splits = jax.random.split(jax.random.key(seed), 7)
    start_block = draw_start_block(jax.random.fold_in(splits[6], 71), 0)
    down_matrix = draw_down_matrix(jax.random.fold_in(splits[6], 71), 0)
    hop_partner = draw_hop_partner(jax.random.fold_in(splits[6], 71), 0)
    hop_sign = draw_hop_sign(jax.random.fold_in(splits[6], 71), 0)
    bond_hop = jnp.clip(jax.random.uniform(splits[4], (BONDS,), jnp.float32, 0.3, 1.0), 0.3, 1.0)
    onsite_u = jnp.clip(jnp.exp(jax.random.uniform(splits[5], (SITES,), jnp.float32, math.log(0.5), math.log(2.0))), 0.5, 2.0)
    return dict(start_block=start_block, down_matrix=down_matrix, hop_partner=hop_partner, hop_sign=hop_sign, bond_hop=bond_hop, onsite_u=onsite_u)


highest = lax.Precision.HIGHEST
center_shift = 6.0
half_range = 12.0

def site_bits(count):
    states = jnp.arange(count, dtype=jnp.int32)
    shifts = jnp.arange(SITES, dtype=jnp.int32)
    return jnp.bitwise_and(jnp.right_shift(states[:, None], shifts[None, :]), 1).astype(jnp.float32)

def apply_hamiltonian(vectors_in, down_matrix, interaction, hop_coef, hop_partner):
    flat_rows = vectors_in.reshape(NU * NVEC, ND)
    result = jnp.dot(flat_rows, down_matrix.T, precision=highest, preferred_element_type=jnp.float32)
    result = result.reshape(NU, NVEC, ND) + interaction[:, None, :] * vectors_in
    for bond_index in range(BONDS):
        result = result + hop_coef[bond_index][:, None, None] * jnp.take(vectors_in, hop_partner[bond_index], axis=0)
    return result

def reference(start_block, down_matrix, hop_partner, hop_sign, bond_hop, onsite_u):
    up_bits = site_bits(NU)
    down_bits = site_bits(ND)
    interaction = jnp.dot(up_bits * onsite_u[None, :], down_bits.T, precision=highest, preferred_element_type=jnp.float32)
    hop_coef = -bond_hop[:, None] * hop_sign.astype(jnp.float32)
    identity = jnp.eye(NVEC, dtype=jnp.float32)
    current = start_block
    for outer_step in range(OUTER):
        previous = current
        for degree_step in range(DEGREE):
            applied = apply_hamiltonian(current, down_matrix, interaction, hop_coef, hop_partner)
            if degree_step == 0:
                following = (applied - center_shift * current) / half_range
            else:
                following = 2.0 * (applied - center_shift * current) / half_range - previous
            previous, current = (current, following)
        gram_sum = jnp.einsum('ukd,uld->kl', current, current, precision=highest)
        norm_scale = 1.0 / jnp.sqrt(jnp.sqrt(jnp.sum(gram_sum * gram_sum)) + 1e-06)
        current = norm_scale * current
        for newton_step in range(NS_ITERS):
            gram_sum = jnp.einsum('ukd,uld->kl', current, current, precision=highest)
            mixing = 1.5 * identity - 0.5 * gram_sum
            current = jnp.einsum('ukd,kl->uld', current, mixing, precision=highest)
    return current * math.sqrt(NU * ND)
```

```python
import functools
import math

import jax
import jax.numpy as jnp
from jax import lax
from jax.experimental import pallas as pl
from jax.experimental.pallas import tpu as pltpu
from jax.sharding import PartitionSpec as P

DEGREE = 2
NS_ITERS = 4
STACK = 4

highest = lax.Precision.HIGHEST
high = lax.Precision.HIGH
center_shift = 6.0
half_range = 12.0


def site_bits(states, sites):
    shifts = jnp.arange(sites, dtype=jnp.int32)
    return jnp.bitwise_and(jnp.right_shift(states[:, None], shifts[None, :]), 1).astype(jnp.float32)


def hop_matrix(hop_coef, hop_partner):
    up_count = hop_partner.shape[1]
    columns = jnp.arange(up_count, dtype=jnp.int32)
    total = jnp.zeros((up_count, up_count), jnp.float32)
    for bond in range(hop_partner.shape[0]):
        total = total + jnp.where(hop_partner[bond][:, None] == columns[None, :], hop_coef[bond][:, None], 0.0)
    return total


def dot(left, right, contract, precision):
    return lax.dot_general(
        left, right, ((contract[:1], contract[1:]), ((), ())), precision=precision, preferred_element_type=jnp.float32
    )


def filter_vector(vector, down_matrix, up_matrix, diagonal, cuts):
    previous, current = vector, vector
    for degree_step in range(DEGREE):
        last = degree_step + 1 == DEGREE
        width = current.shape[1] // (cuts if last else 1)
        pieces = []
        for cut in range(cuts if last else 1):
            columns = slice(cut * width, (cut + 1) * width)
            applied = dot(current, down_matrix[columns], (1, 1), high)
            applied = applied + dot(up_matrix, current[:, columns], (1, 0), high)
            applied = applied + diagonal[:, columns] * current[:, columns]
            if degree_step == 0:
                pieces.append(applied / half_range)
            else:
                pieces.append(2.0 * applied / half_range - previous[:, columns])
        if last:
            return pieces
        previous, current = current, pieces[0]


def spread_step(held, step):
    pairs = [(i, i ^ step) for i in range(lax.axis_size("vec"))]
    return [lax.ppermute(piece, "vec", pairs) for piece in held]


def split(values):
    top = values.astype(jnp.bfloat16)
    return top, (values - top.astype(jnp.float32)).astype(jnp.bfloat16)


def stacked(refs, first, count):
    return jnp.concatenate([ref[first + u] for u in range(count) for ref in refs], axis=0)


def gram_kernel(groups, start_ref, *refs):
    inputs, (top_ref, cross_ref) = refs[:-2], refs[-2:]

    @pl.when(pl.program_id(0) == 0)
    def _():
        top_ref[...] = jnp.zeros_like(top_ref)
        cross_ref[...] = jnp.zeros_like(cross_ref)

    per_group = len(inputs) // groups
    rows = inputs[0].shape[0]
    for first in range(0, rows, STACK):
        for group in range(groups):
            top, low = split(stacked(inputs[group * per_group : (group + 1) * per_group], first, STACK))
            top_ref[...] += dot(top, top, (1, 1), None)
            cross_ref[...] += dot(top, low, (1, 1), None)


def rotate_kernel(groups, mix_ref, *refs):
    inputs, out_ref = refs[:-1], refs[-1]
    per_group = len(inputs) // groups
    rows, width = inputs[0].shape[0], inputs[0].shape[2]
    mix_top, mix_low = split(mix_ref[...])
    count = mix_top.shape[0]
    both = jnp.concatenate([mix_top, mix_low], axis=0)
    for first in range(0, rows, STACK):
        for group in range(groups):
            top, low = split(stacked(inputs[group * per_group : (group + 1) * per_group], first, STACK))
            wide = dot(both, top, (1, 0), None)
            result = wide[:count] + wide[count:] + dot(mix_top, low, (1, 0), None)
            out_ref[first : first + STACK, :, group * width : (group + 1) * width] = result.reshape(
                STACK, count // STACK, width
            )


def gram_partial(groups, start, row_count):
    flat = [array for group in groups for array in group]
    vectors = sum(array.shape[1] for array in groups[0])
    block = min(row_count, 8)
    specs = [pl.BlockSpec((block,) + array.shape[1:], lambda i, first: (first[0] + i, 0, 0)) for array in flat]
    size = STACK * vectors
    out = jax.ShapeDtypeStruct((size, size), jnp.float32)
    top, cross = pl.pallas_call(
        functools.partial(gram_kernel, len(groups)),
        out_shape=(out, out),
        grid_spec=pltpu.PrefetchScalarGridSpec(
            num_scalar_prefetch=1,
            grid=(row_count // block,),
            in_specs=specs,
            out_specs=[pl.BlockSpec((size, size), lambda i, first: (0, 0))] * 2,
        ),
        compiler_params=pltpu.CompilerParams(vmem_limit_bytes=48 * 1024 * 1024),
    )((start * (row_count // block)).reshape(1).astype(jnp.int32), *flat)
    cross = cross + cross.T
    total = (top + cross).reshape(STACK, vectors, STACK, vectors)
    return sum(total[u, :, u, :] for u in range(STACK))


def rotate(groups, mixing, up_local, down_count):
    flat = [array for group in groups for array in group]
    block = 8
    specs = [pl.BlockSpec((block,) + array.shape[1:], lambda i: (i, 0, 0)) for array in flat]
    own = mixing.shape[1]
    wide_mixing = jnp.kron(jnp.eye(STACK, dtype=jnp.float32), mixing.T)
    return pl.pallas_call(
        functools.partial(rotate_kernel, len(groups)),
        out_shape=jax.ShapeDtypeStruct((up_local, own, down_count), jnp.float32),
        grid=(up_local // block,),
        in_specs=[pl.BlockSpec(wide_mixing.shape, lambda i: (0, 0))] + specs,
        out_specs=pl.BlockSpec((block, own, down_count), lambda i: (i, 0, 0)),
        compiler_params=pltpu.CompilerParams(vmem_limit_bytes=48 * 1024 * 1024),
    )(wide_mixing, *flat)


def newton_schulz(gram_sum):
    identity = jnp.eye(gram_sum.shape[0], dtype=jnp.float32)
    norm_scale = 1.0 / jnp.sqrt(jnp.sqrt(jnp.sum(gram_sum * gram_sum)) + 1e-06)
    gram_sum = norm_scale * norm_scale * gram_sum
    product_total = identity
    for _ in range(NS_ITERS):
        mixing = 1.5 * identity - 0.5 * gram_sum
        product_total = dot(product_total, mixing, (1, 0), highest)
        gram_sum = dot(mixing, dot(gram_sum, mixing, (1, 0), highest), (1, 0), highest)
    return norm_scale * product_total


def vector_cut(start_block, down_matrix, hop_coef, hop_partner, onsite_u):
    hil_parts, vec_parts = lax.axis_size("hil"), lax.axis_size("vec")
    up_local, vec_local, down_count = start_block.shape
    up_count = up_local * hil_parts
    rounds = vec_local // hil_parts
    cuts = 2
    arrived = []
    for turn in range(rounds):
        block = start_block[:, turn * hil_parts : (turn + 1) * hil_parts].transpose(1, 0, 2)
        arrived.append(lax.all_to_all(block, "hil", split_axis=0, concat_axis=0, tiled=True))
    up_matrix = hop_matrix(hop_coef, hop_partner)
    sites = onsite_u.shape[0]
    diagonal = -center_shift + jnp.dot(
        site_bits(jnp.arange(up_count, dtype=jnp.int32), sites) * onsite_u[None, :],
        site_bits(jnp.arange(down_count, dtype=jnp.int32), sites).T,
        precision=highest,
        preferred_element_type=jnp.float32,
    )
    sent = []
    for turn in range(rounds):
        vector = arrived[turn].reshape(up_count, down_count)
        for piece in filter_vector(vector, down_matrix, up_matrix, diagonal, cuts):
            piece = piece.reshape(hil_parts, up_local, down_count // cuts)
            now = len(sent)
            for stage, earlier in enumerate(range(now - 2, -1, -1)):
                if stage < len(sent[earlier]) - 1:
                    piece, sent[earlier][stage + 1] = lax.optimization_barrier((piece, sent[earlier][stage + 1]))
            back = lax.all_to_all(piece, "hil", split_axis=0, concat_axis=0, tiled=True)
            sent.append([[back.transpose(1, 0, 2)]])
            step = vec_parts // 2
            while step >= 1:
                sent[now].append(spread_step([p for stage in sent[now] for p in stage], step))
                step //= 2
    groups = [[] for _ in range(cuts)]
    distances = [0]
    step = vec_parts // 2
    while step >= 1:
        distances += [distance ^ step for distance in distances]
        step //= 2
    for number, stages in enumerate(sent):
        held = [piece for stage in stages for piece in stage]
        groups[number % cuts].extend(held[distances.index(distance)] for distance in range(vec_parts))
    own = lax.axis_index("vec")
    near = jnp.bitwise_xor(jnp.arange(vec_parts, dtype=jnp.int32), own)
    exchange = (near[:, None] == jnp.arange(vec_parts, dtype=jnp.int32)[None, :]).astype(jnp.float32)
    order = jnp.kron(jnp.eye(rounds, dtype=jnp.float32), jnp.kron(exchange, jnp.eye(hil_parts, dtype=jnp.float32)))
    partial = gram_partial(groups, own, up_local // vec_parts)
    partial = dot(order, dot(partial, order, (1, 0), highest), (0, 0), highest)
    mixing = newton_schulz(lax.psum(partial, ("hil", "vec")))
    mixing = dot(dot(order, mixing, (1, 0), highest), order, (1, 1), highest)
    mixing = mixing.reshape(-1, rounds, vec_parts, hil_parts)[:, :, 0].reshape(-1, vec_local)
    return rotate(groups, mixing * math.sqrt(up_count * down_count), up_local, down_count)


def split_down(local_block):
    hil_parts = lax.axis_size("hil")
    up_local, vec_local, down_count = local_block.shape
    down_local = down_count // hil_parts
    arranged = local_block.reshape(up_local, vec_local, hil_parts, down_local).transpose(2, 0, 1, 3)
    arranged = arranged.reshape(hil_parts, up_local, vec_local * down_local)
    received = lax.all_to_all(arranged, "hil", split_axis=0, concat_axis=1, tiled=True)
    return received.reshape(hil_parts * up_local, vec_local * down_local)


def split_up(spread, up_local, vec_local):
    hil_parts = lax.axis_size("hil")
    total_up, columns = spread.shape
    down_local = columns // vec_local
    received = lax.all_to_all(
        spread.reshape(1, total_up, columns), "hil", split_axis=1, concat_axis=0, tiled=True
    )
    arranged = received.reshape(hil_parts, up_local, vec_local, down_local).transpose(1, 2, 0, 3)
    return arranged.reshape(up_local, vec_local, hil_parts * down_local)


def advance(applied, present, earlier, degree_step):
    if degree_step == 0:
        return (applied - center_shift * present) / half_range
    return 2.0 * (applied - center_shift * present) / half_range - earlier


def down_cut(start_block, down_matrix, hop_coef, hop_partner, onsite_u):
    up_local, vec_local, down_count = start_block.shape
    up_matrix = hop_matrix(hop_coef, hop_partner)
    sites = onsite_u.shape[0]
    local_states = lax.axis_index("hil") * up_local + jnp.arange(up_local, dtype=jnp.int32)
    interaction = jnp.dot(
        site_bits(local_states, sites) * onsite_u[None, :],
        site_bits(jnp.arange(down_count, dtype=jnp.int32), sites).T,
        precision=highest,
        preferred_element_type=jnp.float32,
    )
    current = previous = start_block
    current_cut = previous_cut = split_down(current)
    for degree_step in range(DEGREE):
        local_part = dot(current.reshape(up_local * vec_local, down_count), down_matrix, (1, 1), high)
        local_part = local_part.reshape(current.shape) + interaction[:, None, :] * current
        hopped = dot(up_matrix, current_cut, (1, 0), high)
        applied = local_part + split_up(hopped, up_local, vec_local)
        following = advance(applied, current, previous, degree_step)
        if degree_step + 1 < DEGREE:
            applied_cut = split_down(local_part) + hopped
            following_cut = advance(applied_cut, current_cut, previous_cut, degree_step)
            previous_cut, current_cut = current_cut, following_cut
        previous, current = current, following
    row_panel = lax.all_to_all(current, "vec", split_axis=2, concat_axis=1, tiled=True)
    gram_sum = lax.psum(jnp.einsum("ukd,uld->kl", row_panel, row_panel, precision=highest), ("hil", "vec"))
    mixing = newton_schulz(gram_sum) * math.sqrt(up_matrix.shape[0] * down_count)
    row_panel = jnp.einsum("ukd,kl->uld", row_panel, mixing, precision=highest)
    return lax.all_to_all(row_panel, "vec", split_axis=1, concat_axis=2, tiled=True)


def on_device(start_block, down_matrix, hop_partner, hop_sign, bond_hop, onsite_u):
    hil_parts, vec_parts = lax.axis_size("hil"), lax.axis_size("vec")
    up_local, vec_local, _ = start_block.shape
    hop_coef = -bond_hop[:, None] * hop_sign.astype(jnp.float32)
    whole_vectors = vec_local % hil_parts == 0 and vec_parts & (vec_parts - 1) == 0
    plan = vector_cut if whole_vectors and up_local % (8 * vec_parts) == 0 else down_cut
    return plan(start_block, down_matrix, hop_coef, hop_partner, onsite_u)


def solution(mesh):
    in_specs = (P("hil", "vec", None), P(), P(), P(), P(), P())
    out_specs = P("hil", "vec", None)
    return jax.shard_map(
        on_device, mesh=mesh, in_specs=in_specs, out_specs=out_specs, check_vma=False
    )
```

```python
import functools
import math

import jax
import jax.numpy as jnp
from jax import lax
from jax.experimental import pallas as pl
from jax.experimental.pallas import tpu as pltpu
from jax.sharding import PartitionSpec as P

DEGREE = 2
NS_ITERS = 4
STACK = 4

highest = lax.Precision.HIGHEST
high = lax.Precision.HIGH
center_shift = 6.0
half_range = 12.0


def site_bits(states, sites):
    shifts = jnp.arange(sites, dtype=jnp.int32)
    return jnp.bitwise_and(jnp.right_shift(states[:, None], shifts[None, :]), 1).astype(jnp.float32)


def hop_matrix(hop_coef, hop_partner):
    up_count = hop_partner.shape[1]
    columns = jnp.arange(up_count, dtype=jnp.int32)
    total = jnp.zeros((up_count, up_count), jnp.float32)
    for bond in range(hop_partner.shape[0]):
        total = total + jnp.where(hop_partner[bond][:, None] == columns[None, :], hop_coef[bond][:, None], 0.0)
    return total


def dot(left, right, contract, precision):
    return lax.dot_general(
        left, right, ((contract[:1], contract[1:]), ((), ())), precision=precision, preferred_element_type=jnp.float32
    )


def apply_rows(vector, vector_rows, down_matrix, up_rows, diagonal_rows):
    applied = dot(vector_rows, down_matrix, (1, 1), high) + dot(up_rows, vector, (1, 0), high)
    return applied + diagonal_rows * vector_rows


def spread_step(held, step):
    pairs = [(i, i ^ step) for i in range(lax.axis_size("vec"))]
    return [lax.ppermute(piece, "vec", pairs) for piece in held]


def split(values):
    top = values.astype(jnp.bfloat16)
    return top, (values - top.astype(jnp.float32)).astype(jnp.bfloat16)


def vectors_first_kernel(start_ref, block_ref, out_ref):
    out_ref[...] = jnp.swapaxes(block_ref[...], 0, 1)


def vectors_first(start_block, turn, count, swapped):
    up_local, _, down_count = start_block.shape
    rows = 16
    blocks = up_local // rows
    return pl.pallas_call(
        vectors_first_kernel,
        out_shape=jax.ShapeDtypeStruct((count, up_local, down_count), jnp.float32),
        grid_spec=pltpu.PrefetchScalarGridSpec(
            num_scalar_prefetch=1,
            grid=(blocks,),
            in_specs=[
                pl.BlockSpec(
                    (rows, count, down_count),
                    lambda i, swap: (lax.rem(i + swap[0] * (blocks // 2), blocks), turn, 0),
                )
            ],
            out_specs=pl.BlockSpec((count, rows, down_count), lambda i, swap: (0, i, 0)),
        ),
        compiler_params=pltpu.CompilerParams(vmem_limit_bytes=56 * 1024 * 1024),
    )(swapped, start_block)


def stacked(refs):
    return jnp.concatenate([jnp.swapaxes(ref[...], 0, 1) for ref in refs], axis=1)


def gram_kernel(start_ref, *refs):
    inputs, (top_ref, cross_ref) = refs[:-2], refs[-2:]

    @pl.when(pl.program_id(0) == 0)
    def _():
        top_ref[...] = jnp.zeros_like(top_ref)
        cross_ref[...] = jnp.zeros_like(cross_ref)

    values = stacked(inputs)
    rows, vectors, columns = values.shape
    for first in range(0, rows, STACK):
        top, low = split(values[first : first + STACK].reshape(STACK * vectors, columns))
        top_ref[...] += dot(top, top, (1, 1), None)
        cross_ref[...] += dot(top, low, (1, 1), None)


def gram_partial(pieces, part, parts):
    vectors = sum(piece.shape[0] for piece in pieces)
    block = 8
    blocks = pieces[0].shape[1] // parts // block
    specs = [
        pl.BlockSpec((piece.shape[0], block, piece.shape[2]), lambda i, first: (0, first[0] + i, 0)) for piece in pieces
    ]
    size = STACK * vectors
    out = jax.ShapeDtypeStruct((size, size), jnp.float32)
    top, cross = pl.pallas_call(
        gram_kernel,
        out_shape=(out, out),
        grid_spec=pltpu.PrefetchScalarGridSpec(
            num_scalar_prefetch=1,
            grid=(blocks,),
            in_specs=specs,
            out_specs=[pl.BlockSpec((size, size), lambda i, first: (0, 0))] * 2,
        ),
        compiler_params=pltpu.CompilerParams(vmem_limit_bytes=48 * 1024 * 1024),
    )((part * blocks).reshape(1), *pieces)
    cross = cross + cross.T
    total = (top + cross).reshape(STACK, vectors, STACK, vectors)
    return sum(total[u, :, u, :] for u in range(STACK))


def rotate_kernel(half_blocks, swap_ref, mix_ref, *refs):
    inputs, out_ref = refs[:-1], refs[-1]
    mix_top, mix_low = split(mix_ref[...])
    count = mix_top.shape[0]
    both = jnp.concatenate([mix_top, mix_low], axis=0)

    def run(half):
        values = stacked(half)
        rows, vectors, columns = values.shape
        for first in range(0, rows, STACK):
            top, low = split(values[first : first + STACK].reshape(STACK * vectors, columns))
            wide = dot(both, top, (1, 0), None)
            result = wide[:count] + wide[count:] + dot(mix_top, low, (1, 0), None)
            out_ref[first : first + STACK] = result.reshape(STACK, count // STACK, result.shape[1])

    pl.when(pl.program_id(0) < half_blocks)(lambda: run(inputs[: len(inputs) // 2]))
    pl.when(pl.program_id(0) >= half_blocks)(lambda: run(inputs[len(inputs) // 2 :]))


def rotate(halves, mixing, swapped):
    half_rows, down_count = halves[0][0].shape[1:]
    block = 8
    half_blocks = half_rows // block
    own = mixing.shape[1]
    wide_mixing = jnp.kron(jnp.eye(STACK, dtype=jnp.float32), mixing.T)
    specs = [pl.BlockSpec(wide_mixing.shape, lambda i, swap: (0, 0))]
    for piece in halves[0]:
        shape = (piece.shape[0], block, down_count)
        specs.append(pl.BlockSpec(shape, lambda i, swap: (0, jnp.minimum(i, half_blocks - 1), 0)))
    for piece in halves[1]:
        shape = (piece.shape[0], block, down_count)
        specs.append(pl.BlockSpec(shape, lambda i, swap: (0, jnp.maximum(i - half_blocks, 0), 0)))
    return pl.pallas_call(
        functools.partial(rotate_kernel, half_blocks),
        out_shape=jax.ShapeDtypeStruct((2 * half_rows, own, down_count), jnp.float32),
        grid_spec=pltpu.PrefetchScalarGridSpec(
            num_scalar_prefetch=1,
            grid=(2 * half_blocks,),
            in_specs=specs,
            out_specs=pl.BlockSpec(
                (block, own, down_count),
                lambda i, swap: (lax.rem(i + swap[0] * half_blocks, 2 * half_blocks), 0, 0),
            ),
        ),
        compiler_params=pltpu.CompilerParams(vmem_limit_bytes=48 * 1024 * 1024),
    )(swapped, wide_mixing, *halves[0], *halves[1])


def newton_schulz(gram_sum):
    identity = jnp.eye(gram_sum.shape[0], dtype=jnp.float32)
    norm_scale = 1.0 / jnp.sqrt(jnp.sqrt(jnp.sum(gram_sum * gram_sum)) + 1e-06)
    gram_sum = norm_scale * norm_scale * gram_sum
    product_total = identity
    for _ in range(NS_ITERS):
        mixing = 1.5 * identity - 0.5 * gram_sum
        product_total = dot(product_total, mixing, (1, 0), highest)
        gram_sum = dot(mixing, dot(gram_sum, mixing, (1, 0), highest), (1, 0), highest)
    return norm_scale * product_total


def vector_cut(start_block, down_matrix, hop_coef, hop_partner, onsite_u):
    hil_parts, vec_parts = lax.axis_size("hil"), lax.axis_size("vec")
    up_local, vec_local, down_count = start_block.shape
    up_count = up_local * hil_parts
    rounds = vec_local // hil_parts
    half_rows = up_local // 2
    side = vec_parts // 2
    own = lax.axis_index("vec")
    swap = own // side
    swapped = swap.reshape(1).astype(jnp.int32)

    def ordered(values):
        cut = values.reshape(values.shape[:-1] + (hil_parts, 2, half_rows))
        return jnp.where(swap == 1, cut[..., ::-1, :], cut).reshape(values.shape)

    arrived = []
    for turn in range(rounds):
        block = vectors_first(start_block, turn, hil_parts, swapped)
        block = lax.all_to_all(block, "hil", split_axis=0, concat_axis=0, tiled=True)
        arrived.append(block.reshape(up_count, down_count))
    other = jnp.where((hop_partner // half_rows) % 2 == 0, hop_partner + half_rows, hop_partner - half_rows)
    up_matrix = hop_matrix(ordered(hop_coef), ordered(jnp.where(swap == 1, other, hop_partner)))
    sites = onsite_u.shape[0]
    diagonal = -center_shift + jnp.dot(
        site_bits(ordered(jnp.arange(up_count, dtype=jnp.int32)), sites) * onsite_u[None, :],
        site_bits(jnp.arange(down_count, dtype=jnp.int32), sites).T,
        precision=highest,
        preferred_element_type=jnp.float32,
    )

    def rows(values, half):
        return values.reshape(hil_parts, 2, half_rows, -1)[:, half].reshape(hil_parts * half_rows, -1)

    def first_step(vector):
        return apply_rows(vector, vector, down_matrix, up_matrix, diagonal) / half_range

    def second_step(vector, before, half):
        applied = apply_rows(vector, rows(vector, half), down_matrix, rows(up_matrix, half), rows(diagonal, half))
        return (2.0 * applied / half_range - rows(before, half)).reshape(hil_parts, half_rows, down_count)

    mine, theirs = 0, 1
    once = first_step(arrived[0])
    crossed = []
    held = [[], []]
    for turn in range(rounds):
        pieces = {half: second_step(once, arrived[turn], half) for half in (theirs, mine)}
        pieces[theirs], pieces[mine] = lax.optimization_barrier((pieces[theirs], pieces[mine]))
        for half in (theirs, mine):
            piece = pieces[half]
            if half == mine and turn + 1 < rounds:
                once = first_step(arrived[turn + 1])
                piece, once = lax.optimization_barrier((piece, once))
            if len(crossed) > 1:
                piece, crossed[-2][0] = lax.optimization_barrier((piece, crossed[-2][0]))
            back = lax.all_to_all(piece, "hil", split_axis=0, concat_axis=0, tiled=True)
            held[half].append(back)
            crossed.append(spread_step([back], side))
    halves = []
    for half in (mine, theirs):
        arrays = []
        for turn in range(rounds):
            near = [held[half][turn], crossed[2 * turn + (0 if half == mine else 1)][0]]
            step = side // 2
            while step >= 1:
                near = near + spread_step(near, step)
                step //= 2
            arrays.extend(near)
        halves.append(arrays)
    distances = [0, side]
    step = side // 2
    while step >= 1:
        distances += [distance ^ step for distance in distances]
        step //= 2
    near = jnp.bitwise_xor(jnp.array(distances, dtype=jnp.int32), own)
    exchange = (near[:, None] == jnp.arange(vec_parts, dtype=jnp.int32)[None, :]).astype(jnp.float32)
    order = jnp.kron(jnp.eye(rounds, dtype=jnp.float32), jnp.kron(exchange, jnp.eye(hil_parts, dtype=jnp.float32)))
    partial = gram_partial(halves[mine], lax.rem(own, side), side)
    partial = dot(order, dot(partial, order, (1, 0), highest), (0, 0), highest)
    mixing = newton_schulz(lax.psum(partial, ("hil", "vec")))
    mixing = dot(dot(order, mixing, (1, 0), highest), order, (1, 1), highest)
    mixing = mixing.reshape(-1, rounds, vec_parts, hil_parts)[:, :, 0].reshape(-1, vec_local)
    return rotate(halves, mixing * math.sqrt(up_count * down_count), swapped)


def split_down(local_block):
    hil_parts = lax.axis_size("hil")
    up_local, vec_local, down_count = local_block.shape
    down_local = down_count // hil_parts
    arranged = local_block.reshape(up_local, vec_local, hil_parts, down_local).transpose(2, 0, 1, 3)
    arranged = arranged.reshape(hil_parts, up_local, vec_local * down_local)
    received = lax.all_to_all(arranged, "hil", split_axis=0, concat_axis=1, tiled=True)
    return received.reshape(hil_parts * up_local, vec_local * down_local)


def split_up(spread, up_local, vec_local):
    hil_parts = lax.axis_size("hil")
    total_up, columns = spread.shape
    down_local = columns // vec_local
    received = lax.all_to_all(
        spread.reshape(1, total_up, columns), "hil", split_axis=1, concat_axis=0, tiled=True
    )
    arranged = received.reshape(hil_parts, up_local, vec_local, down_local).transpose(1, 2, 0, 3)
    return arranged.reshape(up_local, vec_local, hil_parts * down_local)


def advance(applied, present, earlier, degree_step):
    if degree_step == 0:
        return (applied - center_shift * present) / half_range
    return 2.0 * (applied - center_shift * present) / half_range - earlier


def down_cut(start_block, down_matrix, hop_coef, hop_partner, onsite_u):
    up_local, vec_local, down_count = start_block.shape
    up_matrix = hop_matrix(hop_coef, hop_partner)
    sites = onsite_u.shape[0]
    local_states = lax.axis_index("hil") * up_local + jnp.arange(up_local, dtype=jnp.int32)
    interaction = jnp.dot(
        site_bits(local_states, sites) * onsite_u[None, :],
        site_bits(jnp.arange(down_count, dtype=jnp.int32), sites).T,
        precision=highest,
        preferred_element_type=jnp.float32,
    )
    current = previous = start_block
    current_cut = previous_cut = split_down(current)
    for degree_step in range(DEGREE):
        local_part = dot(current.reshape(up_local * vec_local, down_count), down_matrix, (1, 1), high)
        local_part = local_part.reshape(current.shape) + interaction[:, None, :] * current
        hopped = dot(up_matrix, current_cut, (1, 0), high)
        applied = local_part + split_up(hopped, up_local, vec_local)
        following = advance(applied, current, previous, degree_step)
        if degree_step + 1 < DEGREE:
            applied_cut = split_down(local_part) + hopped
            following_cut = advance(applied_cut, current_cut, previous_cut, degree_step)
            previous_cut, current_cut = current_cut, following_cut
        previous, current = current, following
    row_panel = lax.all_to_all(current, "vec", split_axis=2, concat_axis=1, tiled=True)
    gram_sum = lax.psum(jnp.einsum("ukd,uld->kl", row_panel, row_panel, precision=highest), ("hil", "vec"))
    mixing = newton_schulz(gram_sum) * math.sqrt(up_matrix.shape[0] * down_count)
    row_panel = jnp.einsum("ukd,kl->uld", row_panel, mixing, precision=highest)
    return lax.all_to_all(row_panel, "vec", split_axis=1, concat_axis=2, tiled=True)


def on_device(start_block, down_matrix, hop_partner, hop_sign, bond_hop, onsite_u):
    hil_parts, vec_parts = lax.axis_size("hil"), lax.axis_size("vec")
    up_local, vec_local, _ = start_block.shape
    hop_coef = -bond_hop[:, None] * hop_sign.astype(jnp.float32)
    whole_vectors = vec_local % hil_parts == 0 and hil_parts % 8 == 0
    halved = vec_parts > 1 and vec_parts & (vec_parts - 1) == 0 and up_local % (16 * vec_parts) == 0
    plan = vector_cut if whole_vectors and halved else down_cut
    return plan(start_block, down_matrix, hop_coef, hop_partner, onsite_u)


def solution(mesh):
    in_specs = (P("hil", "vec", None), P(), P(), P(), P(), P())
    out_specs = P("hil", "vec", None)
    return jax.shard_map(
        on_device, mesh=mesh, in_specs=in_specs, out_specs=out_specs, check_vma=False
    )
```

```python
import functools
import math

import jax
import jax.numpy as jnp
from jax import lax
from jax.experimental import pallas as pl
from jax.experimental.pallas import tpu as pltpu
from jax.sharding import PartitionSpec as P

DEGREE = 2
NS_ITERS = 4
SUBLANES = 8
STACK = 4

highest = lax.Precision.HIGHEST
high = lax.Precision.HIGH
center_shift = 6.0
half_range = 12.0


def site_bits(states, sites):
    shifts = jnp.arange(sites, dtype=jnp.int32)
    return jnp.bitwise_and(jnp.right_shift(states[:, None], shifts[None, :]), 1).astype(jnp.float32)


def hop_matrix(hop_coef, hop_partner):
    up_count = hop_partner.shape[1]
    columns = jnp.arange(up_count, dtype=jnp.int32)
    total = jnp.zeros((up_count, up_count), jnp.float32)
    for bond in range(hop_partner.shape[0]):
        total = total + jnp.where(hop_partner[bond][:, None] == columns[None, :], hop_coef[bond][:, None], 0.0)
    return total


def dot(left, right, contract, precision):
    return lax.dot_general(
        left, right, ((contract[:1], contract[1:]), ((), ())), precision=precision, preferred_element_type=jnp.float32
    )


def apply_rows(vector, vector_rows, down_matrix, up_rows, diagonal_rows):
    applied = dot(vector_rows, down_matrix, (1, 1), high) + dot(up_rows, vector, (1, 0), high)
    return applied + diagonal_rows * vector_rows


def spread_step(held, step):
    pairs = [(i, i ^ step) for i in range(lax.axis_size("vec"))]
    return [lax.ppermute(piece, "vec", pairs) for piece in held]


def split(values):
    top = values.astype(jnp.bfloat16)
    return top, (values - top.astype(jnp.float32)).astype(jnp.bfloat16)


def vectors_first_kernel(start_ref, block_ref, out_ref):
    out_ref[...] = jnp.swapaxes(block_ref[...], 0, 1)


def vectors_first(start_block, turn, count, swapped):
    up_local, _, down_count = start_block.shape
    rows = 16
    blocks = up_local // rows
    return pl.pallas_call(
        vectors_first_kernel,
        out_shape=jax.ShapeDtypeStruct((count, up_local, down_count), jnp.float32),
        grid_spec=pltpu.PrefetchScalarGridSpec(
            num_scalar_prefetch=1,
            grid=(blocks,),
            in_specs=[
                pl.BlockSpec(
                    (rows, count, down_count),
                    lambda i, swap: (lax.rem(i + swap[0] * (blocks // 2), blocks), turn, 0),
                )
            ],
            out_specs=pl.BlockSpec((count, rows, down_count), lambda i, swap: (0, i, 0)),
        ),
        compiler_params=pltpu.CompilerParams(vmem_limit_bytes=56 * 1024 * 1024),
    )(swapped, start_block)


def stacked(refs):
    return jnp.concatenate([jnp.swapaxes(ref[...], 0, 1) for ref in refs], axis=1)


def gram_kernel(start_ref, *refs):
    inputs, (top_ref, cross_ref) = refs[:-2], refs[-2:]

    @pl.when(pl.program_id(0) == 0)
    def _():
        top_ref[...] = jnp.zeros_like(top_ref)
        cross_ref[...] = jnp.zeros_like(cross_ref)

    values = stacked(inputs)
    rows, vectors, columns = values.shape
    for first in range(0, rows, STACK):
        top, low = split(values[first : first + STACK].reshape(STACK * vectors, columns))
        top_ref[...] += dot(top, top, (1, 1), None)
        cross_ref[...] += dot(top, low, (1, 1), None)


def gram_partial(pieces, part, parts):
    vectors = sum(piece.shape[0] for piece in pieces)
    block = 8
    blocks = pieces[0].shape[1] // parts // block
    specs = [
        pl.BlockSpec((piece.shape[0], block, piece.shape[2]), lambda i, first: (0, first[0] + i, 0)) for piece in pieces
    ]
    size = STACK * vectors
    out = jax.ShapeDtypeStruct((size, size), jnp.float32)
    top, cross = pl.pallas_call(
        gram_kernel,
        out_shape=(out, out),
        grid_spec=pltpu.PrefetchScalarGridSpec(
            num_scalar_prefetch=1,
            grid=(blocks,),
            in_specs=specs,
            out_specs=[pl.BlockSpec((size, size), lambda i, first: (0, 0))] * 2,
        ),
        compiler_params=pltpu.CompilerParams(vmem_limit_bytes=48 * 1024 * 1024),
    )((part * blocks).reshape(1), *pieces)
    cross = cross + cross.T
    total = (top + cross).reshape(STACK, vectors, STACK, vectors)
    return sum(total[u, :, u, :] for u in range(STACK))


def rotate_kernel(swap_ref, mix_ref, *refs):
    inputs, out_ref = [ref for ref in refs[:-1] if ref.ndim == 3 and ref.shape[1] == SUBLANES], refs[-1]
    columns = out_ref.shape[2]
    mix_top, mix_low = split(mix_ref[...])
    count = mix_top.shape[0]
    both = jnp.concatenate([mix_top, mix_low], axis=0)
    top, low = split(jnp.concatenate([ref[...].reshape(-1, columns) for ref in inputs], axis=0))
    wide = dot(both, top, (1, 0), None)
    result = wide[:count] + wide[count:] + dot(mix_top, low, (1, 0), None)
    out_ref[...] = jnp.swapaxes(result.reshape(-1, SUBLANES, columns), 0, 1)


def rotate_half(pieces, wide_mixing, swapped, half, earlier):
    half_rows, down_count = pieces[0].shape[1:]
    blocks = half_rows // SUBLANES
    own = wide_mixing.shape[0] // SUBLANES
    specs = [pl.BlockSpec(wide_mixing.shape, lambda i, swap: (0, 0))]
    for piece in pieces:
        specs.append(pl.BlockSpec((piece.shape[0], SUBLANES, down_count), lambda i, swap: (0, i, 0)))
    operands = [swapped, wide_mixing, *pieces]
    aliases = {}
    if earlier is not None:
        specs.append(pl.BlockSpec(memory_space=pl.ANY))
        aliases = {len(operands): 0}
        operands.append(earlier)
    return pl.pallas_call(
        rotate_kernel,
        out_shape=jax.ShapeDtypeStruct((2 * half_rows, own, down_count), jnp.float32),
        grid_spec=pltpu.PrefetchScalarGridSpec(
            num_scalar_prefetch=1,
            grid=(blocks,),
            in_specs=specs,
            out_specs=pl.BlockSpec(
                (SUBLANES, own, down_count), lambda i, swap: (i + lax.rem(swap[0] + half, 2) * blocks, 0, 0)
            ),
        ),
        input_output_aliases=aliases,
        compiler_params=pltpu.CompilerParams(vmem_limit_bytes=56 * 1024 * 1024),
    )(*operands)


def small_sum(values, axis):
    parts = lax.axis_size(axis)
    if parts & (parts - 1):
        return lax.psum(values, axis)
    step = 1
    while step < parts:
        count = min(4, parts // step)
        moved = []
        for distance in range(step, count * step, step):
            moved.append(lax.ppermute(values, axis, [(i, i ^ distance) for i in range(parts)]))
        for other in moved:
            values = values + other
        step *= count
    return values


def newton_schulz(gram_sum):
    identity = jnp.eye(gram_sum.shape[0], dtype=jnp.float32)
    norm_scale = 1.0 / jnp.sqrt(jnp.sqrt(jnp.sum(gram_sum * gram_sum)) + 1e-06)
    gram_sum = norm_scale * norm_scale * gram_sum
    product_total = identity
    for _ in range(NS_ITERS):
        mixing = 1.5 * identity - 0.5 * gram_sum
        product_total = dot(product_total, mixing, (1, 0), highest)
        gram_sum = dot(mixing, dot(gram_sum, mixing, (1, 0), highest), (1, 0), highest)
    return norm_scale * product_total


def vector_cut(start_block, down_matrix, hop_coef, hop_partner, onsite_u):
    hil_parts, vec_parts = lax.axis_size("hil"), lax.axis_size("vec")
    up_local, vec_local, down_count = start_block.shape
    up_count = up_local * hil_parts
    rounds = vec_local // hil_parts
    half_rows = up_local // 2
    side = vec_parts // 2
    own = lax.axis_index("vec")
    swap = own // side
    swapped = swap.reshape(1).astype(jnp.int32)

    def ordered(values):
        cut = values.reshape(values.shape[:-1] + (hil_parts, 2, half_rows))
        return jnp.where(swap == 1, cut[..., ::-1, :], cut).reshape(values.shape)

    arrived = []
    for turn in range(rounds):
        block = vectors_first(start_block, turn, hil_parts, swapped)
        block = lax.all_to_all(block, "hil", split_axis=0, concat_axis=0, tiled=True)
        arrived.append(block.reshape(up_count, down_count))
    other = jnp.where((hop_partner // half_rows) % 2 == 0, hop_partner + half_rows, hop_partner - half_rows)
    up_matrix = hop_matrix(ordered(hop_coef), ordered(jnp.where(swap == 1, other, hop_partner)))
    sites = onsite_u.shape[0]
    diagonal = -center_shift + jnp.dot(
        site_bits(ordered(jnp.arange(up_count, dtype=jnp.int32)), sites) * onsite_u[None, :],
        site_bits(jnp.arange(down_count, dtype=jnp.int32), sites).T,
        precision=highest,
        preferred_element_type=jnp.float32,
    )

    def rows(values, half):
        return values.reshape(hil_parts, 2, half_rows, -1)[:, half].reshape(hil_parts * half_rows, -1)

    def first_step(vector):
        return apply_rows(vector, vector, down_matrix, up_matrix, diagonal) / half_range

    def second_step(vector, before, half):
        applied = apply_rows(vector, rows(vector, half), down_matrix, rows(up_matrix, half), rows(diagonal, half))
        return (2.0 * applied / half_range - rows(before, half)).reshape(hil_parts, half_rows, down_count)

    mine, theirs = 0, 1
    once = first_step(arrived[0])
    pieces = [second_step(once, arrived[0], half) for half in (mine, theirs)]
    pieces[theirs], pieces[mine] = lax.optimization_barrier((pieces[theirs], pieces[mine]))
    crossed = []
    held = [[], []]
    for turn in range(rounds):
        upcoming = [None, None]
        for half in (theirs, mine):
            piece = pieces[half]
            if half == mine and turn + 1 < rounds:
                once = first_step(arrived[turn + 1])
                upcoming[theirs] = second_step(once, arrived[turn + 1], theirs)
                piece, once, upcoming[theirs] = lax.optimization_barrier((piece, once, upcoming[theirs]))
                upcoming[mine] = second_step(once, arrived[turn + 1], mine)
            if len(crossed) > 1:
                piece, crossed[-2] = lax.optimization_barrier((piece, crossed[-2]))
            back = lax.all_to_all(piece, "hil", split_axis=0, concat_axis=0, tiled=True)
            held[half].append(back)
            crossed.append(spread_step([back], side)[0])
        pieces = upcoming

    def on_side(near):
        step = side // 2
        while step >= 1:
            near = near + spread_step(near, step)
            step //= 2
        return near

    halves = [[], []]
    for turn in range(rounds):
        halves[mine].extend(on_side([held[mine][turn], crossed[2 * turn]]))
    distances = [0, side]
    step = side // 2
    while step >= 1:
        distances += [distance ^ step for distance in distances]
        step //= 2
    near = jnp.bitwise_xor(jnp.array(distances, dtype=jnp.int32), own)
    exchange = (near[:, None] == jnp.arange(vec_parts, dtype=jnp.int32)[None, :]).astype(jnp.float32)
    order = jnp.kron(jnp.eye(rounds, dtype=jnp.float32), jnp.kron(exchange, jnp.eye(hil_parts, dtype=jnp.float32)))
    partial = gram_partial(halves[mine], lax.rem(own, side), side)
    partial = dot(order, dot(partial, order, (1, 0), highest), (0, 0), highest)
    gram_sum = small_sum(small_sum(partial, "vec"), "hil")
    gram_sum, crossed[-1] = lax.optimization_barrier((gram_sum, crossed[-1]))
    for turn in range(rounds):
        halves[theirs].extend(on_side([held[theirs][turn], crossed[2 * turn + 1]]))
    mixing = newton_schulz(gram_sum)
    mixing = dot(dot(order, mixing, (1, 0), highest), order, (1, 1), highest)
    mixing = mixing.reshape(-1, rounds, vec_parts, hil_parts)[:, :, 0].reshape(-1, vec_local)
    mixing = mixing * math.sqrt(up_count * down_count)
    wide_mixing = jnp.kron(mixing.T, jnp.eye(SUBLANES, dtype=jnp.float32))
    result = rotate_half(halves[mine], wide_mixing, swapped, mine, None)
    return rotate_half(halves[theirs], wide_mixing, swapped, theirs, result)


def split_down(local_block):
    hil_parts = lax.axis_size("hil")
    up_local, vec_local, down_count = local_block.shape
    down_local = down_count // hil_parts
    arranged = local_block.reshape(up_local, vec_local, hil_parts, down_local).transpose(2, 0, 1, 3)
    arranged = arranged.reshape(hil_parts, up_local, vec_local * down_local)
    received = lax.all_to_all(arranged, "hil", split_axis=0, concat_axis=1, tiled=True)
    return received.reshape(hil_parts * up_local, vec_local * down_local)


def split_up(spread, up_local, vec_local):
    hil_parts = lax.axis_size("hil")
    total_up, columns = spread.shape
    down_local = columns // vec_local
    received = lax.all_to_all(
        spread.reshape(1, total_up, columns), "hil", split_axis=1, concat_axis=0, tiled=True
    )
    arranged = received.reshape(hil_parts, up_local, vec_local, down_local).transpose(1, 2, 0, 3)
    return arranged.reshape(up_local, vec_local, hil_parts * down_local)


def advance(applied, present, earlier, degree_step):
    if degree_step == 0:
        return (applied - center_shift * present) / half_range
    return 2.0 * (applied - center_shift * present) / half_range - earlier


def down_cut(start_block, down_matrix, hop_coef, hop_partner, onsite_u):
    up_local, vec_local, down_count = start_block.shape
    up_matrix = hop_matrix(hop_coef, hop_partner)
    sites = onsite_u.shape[0]
    local_states = lax.axis_index("hil") * up_local + jnp.arange(up_local, dtype=jnp.int32)
    interaction = jnp.dot(
        site_bits(local_states, sites) * onsite_u[None, :],
        site_bits(jnp.arange(down_count, dtype=jnp.int32), sites).T,
        precision=highest,
        preferred_element_type=jnp.float32,
    )
    current = previous = start_block
    current_cut = previous_cut = split_down(current)
    for degree_step in range(DEGREE):
        local_part = dot(current.reshape(up_local * vec_local, down_count), down_matrix, (1, 1), high)
        local_part = local_part.reshape(current.shape) + interaction[:, None, :] * current
        hopped = dot(up_matrix, current_cut, (1, 0), high)
        applied = local_part + split_up(hopped, up_local, vec_local)
        following = advance(applied, current, previous, degree_step)
        if degree_step + 1 < DEGREE:
            applied_cut = split_down(local_part) + hopped
            following_cut = advance(applied_cut, current_cut, previous_cut, degree_step)
            previous_cut, current_cut = current_cut, following_cut
        previous, current = current, following
    row_panel = lax.all_to_all(current, "vec", split_axis=2, concat_axis=1, tiled=True)
    gram_sum = lax.psum(jnp.einsum("ukd,uld->kl", row_panel, row_panel, precision=highest), ("hil", "vec"))
    mixing = newton_schulz(gram_sum) * math.sqrt(up_matrix.shape[0] * down_count)
    row_panel = jnp.einsum("ukd,kl->uld", row_panel, mixing, precision=highest)
    return lax.all_to_all(row_panel, "vec", split_axis=1, concat_axis=2, tiled=True)


def on_device(start_block, down_matrix, hop_partner, hop_sign, bond_hop, onsite_u):
    hil_parts, vec_parts = lax.axis_size("hil"), lax.axis_size("vec")
    up_local, vec_local, _ = start_block.shape
    hop_coef = -bond_hop[:, None] * hop_sign.astype(jnp.float32)
    whole_vectors = vec_local % hil_parts == 0 and hil_parts % 8 == 0
    halved = vec_parts > 1 and vec_parts & (vec_parts - 1) == 0 and up_local % (16 * vec_parts) == 0
    plan = vector_cut if whole_vectors and halved else down_cut
    return plan(start_block, down_matrix, hop_coef, hop_partner, onsite_u)


def solution(mesh):
    in_specs = (P("hil", "vec", None), P(), P(), P(), P(), P())
    out_specs = P("hil", "vec", None)
    return jax.shard_map(
        on_device, mesh=mesh, in_specs=in_specs, out_specs=out_specs, check_vma=False
    )
```

```python
import functools
import math

import jax
import jax.numpy as jnp
from jax import lax
from jax.experimental import pallas as pl
from jax.experimental.pallas import tpu as pltpu
from jax.sharding import PartitionSpec as P

DEGREE = 2
NS_ITERS = 4
SUBLANES = 8
STACK = 4

highest = lax.Precision.HIGHEST
high = lax.Precision.HIGH
center_shift = 6.0
half_range = 12.0


def site_bits(states, sites):
    shifts = jnp.arange(sites, dtype=jnp.int32)
    return jnp.bitwise_and(jnp.right_shift(states[:, None], shifts[None, :]), 1).astype(jnp.float32)


def hop_matrix(hop_coef, hop_partner):
    up_count = hop_partner.shape[1]
    columns = jnp.arange(up_count, dtype=jnp.int32)
    total = jnp.zeros((up_count, up_count), jnp.float32)
    for bond in range(hop_partner.shape[0]):
        total = total + jnp.where(hop_partner[bond][:, None] == columns[None, :], hop_coef[bond][:, None], 0.0)
    return total


def dot(left, right, contract, precision):
    return lax.dot_general(
        left, right, ((contract[:1], contract[1:]), ((), ())), precision=precision, preferred_element_type=jnp.float32
    )


def apply_rows(vector, vector_rows, down_matrix, up_rows, diagonal_rows):
    applied = dot(vector_rows, down_matrix, (1, 1), high) + dot(up_rows, vector, (1, 0), high)
    return applied + diagonal_rows * vector_rows


def spread_step(held, step):
    pairs = [(i, i ^ step) for i in range(lax.axis_size("vec"))]
    return [lax.ppermute(piece, "vec", pairs) for piece in held]


def split(values):
    top = values.astype(jnp.bfloat16)
    return top, (values - top.astype(jnp.float32)).astype(jnp.bfloat16)


def vectors_first_kernel(place_ref, block_ref, *refs):
    out_refs, scratch_ref = refs[:-1], refs[-1]
    scratch_ref[...] = jnp.swapaxes(block_ref[...], 0, 1)
    for distance, out_ref in enumerate(out_refs):
        out_ref[...] = scratch_ref[jnp.bitwise_xor(place_ref[1], distance)]


def vectors_first(start_block, turn, count, place):
    up_local, _, down_count = start_block.shape
    rows = 16
    blocks = up_local // rows
    return pl.pallas_call(
        vectors_first_kernel,
        out_shape=[jax.ShapeDtypeStruct((up_local, down_count), jnp.float32)] * count,
        grid_spec=pltpu.PrefetchScalarGridSpec(
            num_scalar_prefetch=1,
            grid=(blocks,),
            in_specs=[
                pl.BlockSpec(
                    (rows, count, down_count),
                    lambda i, place: (lax.rem(i + place[0] * (blocks // 2), blocks), turn, 0),
                )
            ],
            out_specs=[pl.BlockSpec((rows, down_count), lambda i, place: (i, 0))] * count,
            scratch_shapes=[pltpu.VMEM((count, rows, down_count), jnp.float32)],
        ),
        compiler_params=pltpu.CompilerParams(vmem_limit_bytes=56 * 1024 * 1024),
    )(place, start_block)


def joined(refs):
    return jnp.concatenate([ref[...] for ref in refs], axis=-1)


def grouped(refs, counts):
    ends = [sum(counts[: i + 1]) for i in range(len(counts))]
    return [refs[end - count : end] for end, count in zip(ends, counts)]


def stacked(refs, counts):
    return jnp.concatenate([jnp.swapaxes(joined(cuts), 0, 1) for cuts in grouped(refs, counts)], axis=1)


def gram_kernel(counts, start_ref, *refs):
    inputs, (top_ref, cross_ref) = refs[:-2], refs[-2:]

    @pl.when(pl.program_id(0) == 0)
    def _():
        top_ref[...] = jnp.zeros_like(top_ref)
        cross_ref[...] = jnp.zeros_like(cross_ref)

    values = stacked(inputs, counts)
    rows, vectors, columns = values.shape
    for first in range(0, rows, STACK):
        top, low = split(values[first : first + STACK].reshape(STACK * vectors, columns))
        top_ref[...] += dot(top, top, (1, 1), None)
        cross_ref[...] += dot(top, low, (1, 1), None)


def gram_partial(pieces, part, parts):
    vectors = sum(cuts[0].shape[0] for cuts in pieces)
    blocks = pieces[0][0].shape[1] // parts // SUBLANES
    flat = [cut for cuts in pieces for cut in cuts]
    specs = [
        pl.BlockSpec((cut.shape[0], SUBLANES, cut.shape[2]), lambda i, first: (0, first[0] + i, 0)) for cut in flat
    ]
    size = STACK * vectors
    out = jax.ShapeDtypeStruct((size, size), jnp.float32)
    top, cross = pl.pallas_call(
        functools.partial(gram_kernel, [len(cuts) for cuts in pieces]),
        out_shape=(out, out),
        grid_spec=pltpu.PrefetchScalarGridSpec(
            num_scalar_prefetch=1,
            grid=(blocks,),
            in_specs=specs,
            out_specs=[pl.BlockSpec((size, size), lambda i, first: (0, 0))] * 2,
        ),
        compiler_params=pltpu.CompilerParams(vmem_limit_bytes=48 * 1024 * 1024),
    )((part * blocks).reshape(1), *flat)
    cross = cross + cross.T
    total = (top + cross).reshape(STACK, vectors, STACK, vectors)
    return sum(total[u, :, u, :] for u in range(STACK))


def rotate_kernel(counts, place_ref, mix_ref, *refs):
    inputs, out_ref = refs[: sum(counts)], refs[-1]
    columns = out_ref.shape[2]
    mix_top, mix_low = split(mix_ref[...])
    count = mix_top.shape[0]
    both = jnp.concatenate([mix_top, mix_low], axis=0)
    top, low = split(jnp.concatenate([joined(cuts).reshape(-1, columns) for cuts in grouped(inputs, counts)], axis=0))
    wide = dot(both, top, (1, 0), None)
    result = wide[:count] + wide[count:] + dot(mix_top, low, (1, 0), None)
    out_ref[...] = jnp.swapaxes(result.reshape(-1, SUBLANES, columns), 0, 1)


def rotate_half(pieces, wide_mixing, place, half, earlier):
    half_rows = pieces[0][0].shape[1]
    down_count = sum(cut.shape[2] for cut in pieces[0])
    blocks = half_rows // SUBLANES
    own = wide_mixing.shape[0] // SUBLANES
    flat = [cut for cuts in pieces for cut in cuts]
    specs = [pl.BlockSpec(wide_mixing.shape, lambda i, place: (0, 0))]
    for cut in flat:
        specs.append(pl.BlockSpec((cut.shape[0], SUBLANES, cut.shape[2]), lambda i, place: (0, i, 0)))
    operands = [place, wide_mixing, *flat]
    aliases = {}
    if earlier is not None:
        specs.append(pl.BlockSpec(memory_space=pl.ANY))
        aliases = {len(operands): 0}
        operands.append(earlier)
    return pl.pallas_call(
        functools.partial(rotate_kernel, [len(cuts) for cuts in pieces]),
        out_shape=jax.ShapeDtypeStruct((2 * half_rows, own, down_count), jnp.float32),
        grid_spec=pltpu.PrefetchScalarGridSpec(
            num_scalar_prefetch=1,
            grid=(blocks,),
            in_specs=specs,
            out_specs=pl.BlockSpec(
                (SUBLANES, own, down_count), lambda i, place: (i + lax.rem(place[0] + half, 2) * blocks, 0, 0)
            ),
        ),
        input_output_aliases=aliases,
        compiler_params=pltpu.CompilerParams(vmem_limit_bytes=56 * 1024 * 1024),
    )(*operands)


def small_sum(values, axis):
    parts = lax.axis_size(axis)
    if parts & (parts - 1):
        return lax.psum(values, axis)
    step = 1
    while step < parts:
        count = min(4, parts // step)
        moved = []
        for distance in range(step, count * step, step):
            moved.append(lax.ppermute(values, axis, [(i, i ^ distance) for i in range(parts)]))
        for other in moved:
            values = values + other
        step *= count
    return values


def newton_schulz(gram_sum):
    identity = jnp.eye(gram_sum.shape[0], dtype=jnp.float32)
    norm_scale = 1.0 / jnp.sqrt(jnp.sqrt(jnp.sum(gram_sum * gram_sum)) + 1e-06)
    gram_sum = norm_scale * norm_scale * gram_sum
    product_total = identity
    for _ in range(NS_ITERS):
        mixing = 1.5 * identity - 0.5 * gram_sum
        product_total = dot(product_total, mixing, (1, 0), highest)
        gram_sum = dot(mixing, dot(gram_sum, mixing, (1, 0), highest), (1, 0), highest)
    return norm_scale * product_total


def after(value, cell):
    value, cell[0] = lax.optimization_barrier((value, cell[0]))
    return value


def vector_cut(start_block, down_matrix, hop_coef, hop_partner, onsite_u):
    hil_parts, vec_parts = lax.axis_size("hil"), lax.axis_size("vec")
    up_local, vec_local, down_count = start_block.shape
    up_count = up_local * hil_parts
    rounds = vec_local // hil_parts
    half_rows = up_local // 2
    side = vec_parts // 2
    row, own = lax.axis_index("hil"), lax.axis_index("vec")
    swap = own // side
    place = jnp.stack([swap, row]).astype(jnp.int32)

    def ordered(values):
        lead = values.shape[:-1]
        cut = values.reshape(lead + (hil_parts, 2, half_rows))
        cut = jnp.where(swap == 1, cut[..., ::-1, :], cut)
        step = 1
        while step < hil_parts:
            cut = cut.reshape(lead + (hil_parts // step // 2, 2, step * up_local))
            cut = jnp.where((row // step) % 2 == 1, cut[..., ::-1, :], cut)
            step *= 2
        return cut.reshape(values.shape)

    def position(states):
        inner = states % up_local
        inner = jnp.where(swap == 1, jnp.where(inner < half_rows, inner + half_rows, inner - half_rows), inner)
        return jnp.bitwise_xor(states // up_local, row) * up_local + inner

    flight = 2 * 1024 * 1024
    sent = []

    def send(blocks, extra):
        cells = [[blocks[0]]] + [None] * (hil_parts - 1)
        order = []
        far, near = list(range(hil_parts - 1, hil_parts // 2 - 1, -1)), list(range(hil_parts // 2 - 1, 0, -1))
        while far or near:
            order += far[:1] + near[:1]
            far, near = far[1:], near[1:]
        for number, distance in enumerate(order):
            block = blocks[distance]
            size = 4 * block.size
            ahead, waiting = 0, len(sent)
            while waiting > 0 and ahead + size <= flight:
                waiting -= 1
                ahead += 4 * sent[waiting][0].size
            if waiting > 0:
                block = after(block, sent[waiting - 1])
            if number == len(order) // 2 and extra is not None:
                block = after(block, extra)
            cell = [lax.ppermute(block, "hil", [(i, i ^ distance) for i in range(hil_parts)])]
            sent.append(cell)
            cells[distance] = cell
        return cells

    inward = [send(vectors_first(start_block, turn, hil_parts, place), None) for turn in range(rounds)]
    arrived = [jnp.concatenate([cell[0] for cell in cells], axis=0) for cells in inward]
    up_matrix = hop_matrix(ordered(hop_coef), ordered(position(hop_partner)))
    sites = onsite_u.shape[0]
    diagonal = -center_shift + jnp.dot(
        site_bits(ordered(jnp.arange(up_count, dtype=jnp.int32)), sites) * onsite_u[None, :],
        site_bits(jnp.arange(down_count, dtype=jnp.int32), sites).T,
        precision=highest,
        preferred_element_type=jnp.float32,
    )

    def rows(values, half):
        return values.reshape(hil_parts, 2, half_rows, -1)[:, half].reshape(hil_parts * half_rows, -1)

    def first_step(vector):
        return apply_rows(vector, vector, down_matrix, up_matrix, diagonal) / half_range

    def second_step(vector, before, half):
        applied = apply_rows(vector, rows(vector, half), down_matrix, rows(up_matrix, half), rows(diagonal, half))
        return (2.0 * applied / half_range - rows(before, half)).reshape(hil_parts, half_rows, down_count)

    mine, theirs = 0, 1
    once = first_step(arrived[0])
    pieces = [second_step(once, arrived[0], half) for half in (mine, theirs)]
    pieces[theirs], pieces[mine] = lax.optimization_barrier((pieces[theirs], pieces[mine]))
    work = []
    for turn in range(rounds):
        upcoming = [None, None]
        for half in (theirs, mine):
            piece = pieces[half]
            if half == mine and turn + 1 < rounds:
                once = first_step(arrived[turn + 1])
                upcoming[theirs] = second_step(once, arrived[turn + 1], theirs)
                piece, once, upcoming[theirs] = lax.optimization_barrier((piece, once, upcoming[theirs]))
                upcoming[mine] = second_step(once, arrived[turn + 1], mine)
            cuts = 2 if (turn, half) in ((0, theirs), (rounds - 1, mine)) else 1
            width = down_count // cuts
            for cut in range(cuts):
                blocks = [piece[distance, :, cut * width : (cut + 1) * width] for distance in range(hil_parts)]
                extra = work[-2][3] if len(work) > 1 else None
                back = jnp.stack([cell[0] for cell in send(blocks, extra)])
                last = (turn, half, cut) == (rounds - 1, mine, cuts - 1)
                work.append((half, turn, back, [None if last else spread_step([back], side)[0]]))
        pieces = upcoming

    def on_side(near):
        step = side // 2
        while step >= 1:
            near = near + spread_step(near, step)
            step //= 2
        return near

    def gathered(half):
        result = []
        for turn in range(rounds):
            here = [on_side([back]) for h, t, back, _ in work if (h, t) == (half, turn)]
            there = [on_side([cell[0]]) for h, t, _, cell in work if (h, t) == (1 - half, turn)]
            result += [list(cuts) for cuts in zip(*here)]
            result += [list(cuts) for cuts in zip(*there)]
        return result

    step, distances = side // 2, [0]
    while step >= 1:
        distances += [distance ^ step for distance in distances]
        step //= 2
    distances += [distance ^ side for distance in distances]
    near = jnp.bitwise_xor(jnp.array(distances, dtype=jnp.int32), own)
    over_vec = (near[:, None] == jnp.arange(vec_parts, dtype=jnp.int32)[None, :]).astype(jnp.float32)
    near = jnp.bitwise_xor(jnp.arange(hil_parts, dtype=jnp.int32), row)
    over_hil = (near[:, None] == jnp.arange(hil_parts, dtype=jnp.int32)[None, :]).astype(jnp.float32)
    turns = jnp.eye(rounds, dtype=jnp.float32)
    order = jnp.kron(turns, jnp.kron(over_vec, over_hil))
    order_out = jnp.kron(turns, jnp.kron(over_vec, jnp.eye(hil_parts, dtype=jnp.float32)))
    order_out = order_out.reshape(rounds, vec_parts, hil_parts, -1)[:, 0].reshape(vec_local, -1)
    own_pieces = gathered(mine)
    partial = gram_partial(own_pieces, lax.rem(own, side), side)
    partial = dot(order, dot(partial, order, (1, 0), highest), (0, 0), highest)
    partial = small_sum(partial, "vec")
    back, partial = lax.optimization_barrier((work[-1][2], partial))
    work[-1][3][0] = spread_step([back], side)[0]
    mixing = newton_schulz(small_sum(partial, "hil")) * math.sqrt(up_count * down_count)
    mixing = dot(dot(order_out, mixing, (1, 1), highest), order, (1, 1), highest)
    wide = jnp.arange(vec_local * SUBLANES, dtype=jnp.int32)
    long = jnp.arange(order.shape[0] * SUBLANES, dtype=jnp.int32)
    left = (wide[:, None] // SUBLANES == jnp.arange(vec_local, dtype=jnp.int32)[None, :]).astype(jnp.float32)
    right = (jnp.arange(order.shape[0], dtype=jnp.int32)[:, None] == long[None, :] // SUBLANES).astype(jnp.float32)
    wide_mixing = dot(left, dot(mixing, right, (1, 0), highest), (1, 0), highest)
    wide_mixing = jnp.where(wide[:, None] % SUBLANES == long[None, :] % SUBLANES, wide_mixing, 0.0)
    result = rotate_half(own_pieces, wide_mixing, place, mine, None)
    return rotate_half(gathered(theirs), wide_mixing, place, theirs, result)


def split_down(local_block):
    hil_parts = lax.axis_size("hil")
    up_local, vec_local, down_count = local_block.shape
    down_local = down_count // hil_parts
    arranged = local_block.reshape(up_local, vec_local, hil_parts, down_local).transpose(2, 0, 1, 3)
    arranged = arranged.reshape(hil_parts, up_local, vec_local * down_local)
    received = lax.all_to_all(arranged, "hil", split_axis=0, concat_axis=1, tiled=True)
    return received.reshape(hil_parts * up_local, vec_local * down_local)


def split_up(spread, up_local, vec_local):
    hil_parts = lax.axis_size("hil")
    total_up, columns = spread.shape
    down_local = columns // vec_local
    received = lax.all_to_all(
        spread.reshape(1, total_up, columns), "hil", split_axis=1, concat_axis=0, tiled=True
    )
    arranged = received.reshape(hil_parts, up_local, vec_local, down_local).transpose(1, 2, 0, 3)
    return arranged.reshape(up_local, vec_local, hil_parts * down_local)


def advance(applied, present, earlier, degree_step):
    if degree_step == 0:
        return (applied - center_shift * present) / half_range
    return 2.0 * (applied - center_shift * present) / half_range - earlier


def down_cut(start_block, down_matrix, hop_coef, hop_partner, onsite_u):
    up_local, vec_local, down_count = start_block.shape
    up_matrix = hop_matrix(hop_coef, hop_partner)
    sites = onsite_u.shape[0]
    local_states = lax.axis_index("hil") * up_local + jnp.arange(up_local, dtype=jnp.int32)
    interaction = jnp.dot(
        site_bits(local_states, sites) * onsite_u[None, :],
        site_bits(jnp.arange(down_count, dtype=jnp.int32), sites).T,
        precision=highest,
        preferred_element_type=jnp.float32,
    )
    current = previous = start_block
    current_cut = previous_cut = split_down(current)
    for degree_step in range(DEGREE):
        local_part = dot(current.reshape(up_local * vec_local, down_count), down_matrix, (1, 1), high)
        local_part = local_part.reshape(current.shape) + interaction[:, None, :] * current
        hopped = dot(up_matrix, current_cut, (1, 0), high)
        applied = local_part + split_up(hopped, up_local, vec_local)
        following = advance(applied, current, previous, degree_step)
        if degree_step + 1 < DEGREE:
            applied_cut = split_down(local_part) + hopped
            following_cut = advance(applied_cut, current_cut, previous_cut, degree_step)
            previous_cut, current_cut = current_cut, following_cut
        previous, current = current, following
    row_panel = lax.all_to_all(current, "vec", split_axis=2, concat_axis=1, tiled=True)
    gram_sum = lax.psum(jnp.einsum("ukd,uld->kl", row_panel, row_panel, precision=highest), ("hil", "vec"))
    mixing = newton_schulz(gram_sum) * math.sqrt(up_matrix.shape[0] * down_count)
    row_panel = jnp.einsum("ukd,kl->uld", row_panel, mixing, precision=highest)
    return lax.all_to_all(row_panel, "vec", split_axis=1, concat_axis=2, tiled=True)


def on_device(start_block, down_matrix, hop_partner, hop_sign, bond_hop, onsite_u):
    hil_parts, vec_parts = lax.axis_size("hil"), lax.axis_size("vec")
    up_local, vec_local, _ = start_block.shape
    hop_coef = -bond_hop[:, None] * hop_sign.astype(jnp.float32)
    whole_vectors = vec_local % hil_parts == 0 and hil_parts % 8 == 0 and hil_parts & (hil_parts - 1) == 0
    halved = vec_parts > 1 and vec_parts & (vec_parts - 1) == 0 and up_local % (16 * vec_parts) == 0
    plan = vector_cut if whole_vectors and halved else down_cut
    return plan(start_block, down_matrix, hop_coef, hop_partner, onsite_u)


def solution(mesh):
    in_specs = (P("hil", "vec", None), P(), P(), P(), P(), P())
    out_specs = P("hil", "vec", None)
    return jax.shard_map(
        on_device, mesh=mesh, in_specs=in_specs, out_specs=out_specs, check_vma=False
    )
```

```python
import functools
import math

import jax
import jax.numpy as jnp
from jax import lax
from jax.experimental import pallas as pl
from jax.experimental.pallas import tpu as pltpu
from jax.sharding import PartitionSpec as P

DEGREE = 2
NS_ITERS = 4
SUBLANES = 8
STACK = 4

highest = lax.Precision.HIGHEST
high = lax.Precision.HIGH
center_shift = 6.0
half_range = 12.0


def site_bits(states, sites):
    shifts = jnp.arange(sites, dtype=jnp.int32)
    return jnp.bitwise_and(jnp.right_shift(states[:, None], shifts[None, :]), 1).astype(jnp.float32)


def hop_matrix(hop_coef, hop_partner):
    up_count = hop_partner.shape[1]
    columns = jnp.arange(up_count, dtype=jnp.int32)
    total = jnp.zeros((up_count, up_count), jnp.float32)
    for bond in range(hop_partner.shape[0]):
        total = total + jnp.where(hop_partner[bond][:, None] == columns[None, :], hop_coef[bond][:, None], 0.0)
    return total


def dot(left, right, contract, precision):
    return lax.dot_general(
        left, right, ((contract[:1], contract[1:]), ((), ())), precision=precision, preferred_element_type=jnp.float32
    )


def apply_rows(vector, vector_rows, down_matrix, up_rows, diagonal_rows):
    applied = dot(vector_rows, down_matrix, (1, 1), high) + dot(up_rows, vector, (1, 0), high)
    return applied + diagonal_rows * vector_rows


def spread_step(held, step):
    pairs = [(i, i ^ step) for i in range(lax.axis_size("vec"))]
    return [lax.ppermute(piece, "vec", pairs) for piece in held]


def split(values):
    top = values.astype(jnp.bfloat16)
    return top, (values - top.astype(jnp.float32)).astype(jnp.bfloat16)


def vectors_first_kernel(place_ref, block_ref, out_ref):
    out_ref[...] = jnp.swapaxes(block_ref[...], 0, 1)


def vectors_first(start_block, turn, count, place):
    up_local, _, down_count = start_block.shape
    rows = 16
    blocks = up_local // rows
    return pl.pallas_call(
        vectors_first_kernel,
        out_shape=jax.ShapeDtypeStruct((count, up_local, down_count), jnp.float32),
        grid_spec=pltpu.PrefetchScalarGridSpec(
            num_scalar_prefetch=1,
            grid=(blocks,),
            in_specs=[
                pl.BlockSpec(
                    (rows, count, down_count),
                    lambda i, place: (lax.rem(i + place[0] * (blocks // 2), blocks), turn, 0),
                )
            ],
            out_specs=pl.BlockSpec((count, rows, down_count), lambda i, place: (0, i, 0)),
        ),
        compiler_params=pltpu.CompilerParams(vmem_limit_bytes=56 * 1024 * 1024),
    )(place, start_block)


def joined(refs):
    return jnp.concatenate([ref[...] for ref in refs], axis=-1)


def grouped(refs, counts):
    ends = [sum(counts[: i + 1]) for i in range(len(counts))]
    return [refs[end - count : end] for end, count in zip(ends, counts)]


def stacked(refs, counts):
    return jnp.concatenate([jnp.swapaxes(joined(cuts), 0, 1) for cuts in grouped(refs, counts)], axis=1)


def gram_kernel(counts, start_ref, *refs):
    inputs, (top_ref, cross_ref) = refs[:-2], refs[-2:]

    @pl.when(pl.program_id(0) == 0)
    def _():
        top_ref[...] = jnp.zeros_like(top_ref)
        cross_ref[...] = jnp.zeros_like(cross_ref)

    values = stacked(inputs, counts)
    rows, vectors, columns = values.shape
    for first in range(0, rows, STACK):
        top, low = split(values[first : first + STACK].reshape(STACK * vectors, columns))
        top_ref[...] += dot(top, top, (1, 1), None)
        cross_ref[...] += dot(top, low, (1, 1), None)


def gram_partial(pieces, part, parts):
    vectors = sum(cuts[0].shape[0] for cuts in pieces)
    blocks = pieces[0][0].shape[1] // parts // SUBLANES
    flat = [cut for cuts in pieces for cut in cuts]
    specs = [
        pl.BlockSpec((cut.shape[0], SUBLANES, cut.shape[2]), lambda i, first: (0, first[0] + i, 0)) for cut in flat
    ]
    size = STACK * vectors
    out = jax.ShapeDtypeStruct((size, size), jnp.float32)
    top, cross = pl.pallas_call(
        functools.partial(gram_kernel, [len(cuts) for cuts in pieces]),
        out_shape=(out, out),
        grid_spec=pltpu.PrefetchScalarGridSpec(
            num_scalar_prefetch=1,
            grid=(blocks,),
            in_specs=specs,
            out_specs=[pl.BlockSpec((size, size), lambda i, first: (0, 0))] * 2,
        ),
        compiler_params=pltpu.CompilerParams(vmem_limit_bytes=48 * 1024 * 1024),
        cost_estimate=pl.CostEstimate(
            flops=4 * size * size * flat[0].shape[2] * blocks * SUBLANES // STACK,
            bytes_accessed=4 * sum(cut.size for cut in flat) // parts,
            transcendentals=0,
        ),
    )((part * blocks).reshape(1), *flat)
    cross = cross + cross.T
    total = (top + cross).reshape(STACK, vectors, STACK, vectors)
    return sum(total[u, :, u, :] for u in range(STACK))


def rotate_kernel(counts, place_ref, mix_ref, *refs):
    inputs, out_ref = refs[: sum(counts)], refs[-1]
    columns = out_ref.shape[2]
    mix_top, mix_low = split(mix_ref[...])
    count = mix_top.shape[0]
    both = jnp.concatenate([mix_top, mix_low], axis=0)
    top, low = split(jnp.concatenate([joined(cuts).reshape(-1, columns) for cuts in grouped(inputs, counts)], axis=0))
    wide = dot(both, top, (1, 0), None)
    result = wide[:count] + wide[count:] + dot(mix_top, low, (1, 0), None)
    out_ref[...] = result.reshape(SUBLANES, -1, columns)


def rotate_half(pieces, wide_mixing, place, half, earlier):
    half_rows = pieces[0][0].shape[1]
    down_count = sum(cut.shape[2] for cut in pieces[0])
    blocks = half_rows // SUBLANES
    own = wide_mixing.shape[0] // SUBLANES
    flat = [cut for cuts in pieces for cut in cuts]
    specs = [pl.BlockSpec(wide_mixing.shape, lambda i, place: (0, 0))]
    for cut in flat:
        specs.append(pl.BlockSpec((cut.shape[0], SUBLANES, cut.shape[2]), lambda i, place: (0, i, 0)))
    operands = [place, wide_mixing, *flat]
    aliases = {}
    if earlier is not None:
        specs.append(pl.BlockSpec(memory_space=pl.ANY))
        aliases = {len(operands): 0}
        operands.append(earlier)
    return pl.pallas_call(
        functools.partial(rotate_kernel, [len(cuts) for cuts in pieces]),
        out_shape=jax.ShapeDtypeStruct((2 * half_rows, own, down_count), jnp.float32),
        grid_spec=pltpu.PrefetchScalarGridSpec(
            num_scalar_prefetch=1,
            grid=(blocks,),
            in_specs=specs,
            out_specs=pl.BlockSpec(
                (SUBLANES, own, down_count), lambda i, place: (i + lax.rem(place[0] + half, 2) * blocks, 0, 0)
            ),
        ),
        input_output_aliases=aliases,
        compiler_params=pltpu.CompilerParams(vmem_limit_bytes=56 * 1024 * 1024),
        cost_estimate=pl.CostEstimate(
            flops=6 * wide_mixing.size * down_count * blocks,
            bytes_accessed=4 * (sum(cut.size for cut in flat) + half_rows * own * down_count),
            transcendentals=0,
        ),
    )(*operands)


def small_sum(values, axis):
    parts = lax.axis_size(axis)
    if parts & (parts - 1):
        return lax.psum(values, axis)
    step = 1
    while step < parts:
        count = min(4, parts // step)
        moved = []
        for distance in range(step, count * step, step):
            moved.append(lax.ppermute(values, axis, [(i, i ^ distance) for i in range(parts)]))
        for other in moved:
            values = values + other
        step *= count
    return values


def newton_schulz(gram_sum):
    identity = jnp.eye(gram_sum.shape[0], dtype=jnp.float32)
    norm_scale = 1.0 / jnp.sqrt(jnp.sqrt(jnp.sum(gram_sum * gram_sum)) + 1e-06)
    gram_sum = norm_scale * norm_scale * gram_sum
    product_total = identity
    for _ in range(NS_ITERS):
        mixing = 1.5 * identity - 0.5 * gram_sum
        product_total = dot(product_total, mixing, (1, 0), highest)
        gram_sum = dot(mixing, dot(gram_sum, mixing, (1, 0), highest), (1, 0), highest)
    return norm_scale * product_total


def vector_cut(start_block, down_matrix, hop_coef, hop_partner, onsite_u):
    hil_parts, vec_parts = lax.axis_size("hil"), lax.axis_size("vec")
    up_local, vec_local, down_count = start_block.shape
    up_count = up_local * hil_parts
    rounds = vec_local // hil_parts
    half_rows = up_local // 2
    side = vec_parts // 2
    own = lax.axis_index("vec")
    swap = own // side
    place = swap.reshape(1).astype(jnp.int32)

    def ordered(values):
        cut = values.reshape(values.shape[:-1] + (hil_parts, 2, half_rows))
        return jnp.where(swap == 1, cut[..., ::-1, :], cut).reshape(values.shape)

    arrived = []
    for turn in range(rounds):
        block = vectors_first(start_block, turn, hil_parts, place)
        block = lax.all_to_all(block, "hil", split_axis=0, concat_axis=0, tiled=True)
        arrived.append(block.reshape(up_count, down_count))
    other = jnp.where((hop_partner // half_rows) % 2 == 0, hop_partner + half_rows, hop_partner - half_rows)
    up_matrix = hop_matrix(ordered(hop_coef), ordered(jnp.where(swap == 1, other, hop_partner)))
    sites = onsite_u.shape[0]
    diagonal = -center_shift + jnp.dot(
        site_bits(ordered(jnp.arange(up_count, dtype=jnp.int32)), sites) * onsite_u[None, :],
        site_bits(jnp.arange(down_count, dtype=jnp.int32), sites).T,
        precision=highest,
        preferred_element_type=jnp.float32,
    )

    def rows(values, half):
        return values.reshape(hil_parts, 2, half_rows, -1)[:, half].reshape(hil_parts * half_rows, -1)

    def first_step(vector):
        return apply_rows(vector, vector, down_matrix, up_matrix, diagonal) / half_range

    def second_step(vector, before, half):
        applied = apply_rows(vector, rows(vector, half), down_matrix, rows(up_matrix, half), rows(diagonal, half))
        return (2.0 * applied / half_range - rows(before, half)).reshape(hil_parts, half_rows, down_count)

    mine, theirs = 0, 1
    once = first_step(arrived[0])
    pieces = [second_step(once, arrived[0], half) for half in (mine, theirs)]
    pieces[theirs], pieces[mine] = lax.optimization_barrier((pieces[theirs], pieces[mine]))
    crossed = []
    held = [[], []]
    for turn in range(rounds):
        upcoming = [None, None]
        for half in (theirs, mine):
            piece = pieces[half]
            if half == mine and turn + 1 < rounds:
                once = first_step(arrived[turn + 1])
                upcoming[theirs] = second_step(once, arrived[turn + 1], theirs)
                piece, once, upcoming[theirs] = lax.optimization_barrier((piece, once, upcoming[theirs]))
                upcoming[mine] = second_step(once, arrived[turn + 1], mine)
            if len(crossed) > 1:
                piece, crossed[-2] = lax.optimization_barrier((piece, crossed[-2]))
            back = lax.all_to_all(piece, "hil", split_axis=0, concat_axis=0, tiled=True)
            held[half].append(back)
            if (turn, half) == (rounds - 1, mine):
                bounds = [0, down_count // 4, down_count // 8 * 5, down_count]
                cuts = [back[:, :, begin:end] for begin, end in zip(bounds, bounds[1:])]
                crossed.append(spread_step(cuts[:1], side)[0])
            else:
                crossed.append(spread_step([back], side)[0])
        pieces = upcoming

    def on_side(near):
        step = side // 2
        while step >= 1:
            near = near + spread_step(near, step)
            step //= 2
        return near

    own_pieces = []
    for turn in range(rounds):
        own_pieces += [[piece] for piece in on_side([held[mine][turn]]) + on_side([crossed[2 * turn]])]
    step, distances = side // 2, [0]
    while step >= 1:
        distances += [distance ^ step for distance in distances]
        step //= 2
    distances += [distance ^ side for distance in distances]
    near = jnp.bitwise_xor(jnp.array(distances, dtype=jnp.int32), own)
    exchange = (near[:, None] == jnp.arange(vec_parts, dtype=jnp.int32)[None, :]).astype(jnp.float32)
    order = jnp.kron(jnp.eye(rounds, dtype=jnp.float32), jnp.kron(exchange, jnp.eye(hil_parts, dtype=jnp.float32)))
    order_own = order.reshape(rounds, vec_parts, hil_parts, -1)[:, 0].reshape(vec_local, -1)
    partial = gram_partial(own_pieces, lax.rem(own, side), side)
    partial = dot(order, dot(partial, order, (1, 0), highest), (0, 0), highest)
    partial, cuts[0] = lax.optimization_barrier((partial, crossed[-1]))
    partial, cuts[1] = lax.optimization_barrier((small_sum(partial, "vec"), cuts[1]))
    cuts[1] = spread_step(cuts[1:2], side)[0]
    gram_sum, cuts[1], cuts[2] = lax.optimization_barrier((small_sum(partial, "hil"), cuts[1], cuts[2]))
    cuts[2] = spread_step(cuts[2:], side)[0]
    mixing = newton_schulz(gram_sum) * math.sqrt(up_count * down_count)
    mixing = dot(dot(order_own, mixing, (1, 1), highest), order, (1, 1), highest)
    wide = jnp.arange(vec_local * SUBLANES, dtype=jnp.int32)
    long = jnp.arange(order.shape[0] * SUBLANES, dtype=jnp.int32)
    left = (wide[:, None] % vec_local == jnp.arange(vec_local, dtype=jnp.int32)[None, :]).astype(jnp.float32)
    right = (jnp.arange(order.shape[0], dtype=jnp.int32)[:, None] == long[None, :] // SUBLANES).astype(jnp.float32)
    wide_mixing = dot(left, dot(mixing, right, (1, 0), highest), (1, 0), highest)
    wide_mixing = jnp.where(wide[:, None] // vec_local == long[None, :] % SUBLANES, wide_mixing, 0.0)
    result = rotate_half(own_pieces, wide_mixing, place, mine, None)
    result, cuts[2] = lax.optimization_barrier((result, cuts[2]))
    other_pieces = []
    for turn in range(rounds):
        there = cuts if turn == rounds - 1 else [crossed[2 * turn + 1]]
        here = [[piece] for piece in on_side([held[theirs][turn]])]
        there = [list(group) for group in zip(*[on_side([cut]) for cut in there])]
        other_pieces += here + there
    return rotate_half(other_pieces, wide_mixing, place, theirs, result)


def split_down(local_block):
    hil_parts = lax.axis_size("hil")
    up_local, vec_local, down_count = local_block.shape
    down_local = down_count // hil_parts
    arranged = local_block.reshape(up_local, vec_local, hil_parts, down_local).transpose(2, 0, 1, 3)
    arranged = arranged.reshape(hil_parts, up_local, vec_local * down_local)
    received = lax.all_to_all(arranged, "hil", split_axis=0, concat_axis=1, tiled=True)
    return received.reshape(hil_parts * up_local, vec_local * down_local)


def split_up(spread, up_local, vec_local):
    hil_parts = lax.axis_size("hil")
    total_up, columns = spread.shape
    down_local = columns // vec_local
    received = lax.all_to_all(
        spread.reshape(1, total_up, columns), "hil", split_axis=1, concat_axis=0, tiled=True
    )
    arranged = received.reshape(hil_parts, up_local, vec_local, down_local).transpose(1, 2, 0, 3)
    return arranged.reshape(up_local, vec_local, hil_parts * down_local)


def advance(applied, present, earlier, degree_step):
    if degree_step == 0:
        return (applied - center_shift * present) / half_range
    return 2.0 * (applied - center_shift * present) / half_range - earlier


def down_cut(start_block, down_matrix, hop_coef, hop_partner, onsite_u):
    up_local, vec_local, down_count = start_block.shape
    up_matrix = hop_matrix(hop_coef, hop_partner)
    sites = onsite_u.shape[0]
    local_states = lax.axis_index("hil") * up_local + jnp.arange(up_local, dtype=jnp.int32)
    interaction = jnp.dot(
        site_bits(local_states, sites) * onsite_u[None, :],
        site_bits(jnp.arange(down_count, dtype=jnp.int32), sites).T,
        precision=highest,
        preferred_element_type=jnp.float32,
    )
    current = previous = start_block
    current_cut = previous_cut = split_down(current)
    for degree_step in range(DEGREE):
        local_part = dot(current.reshape(up_local * vec_local, down_count), down_matrix, (1, 1), high)
        local_part = local_part.reshape(current.shape) + interaction[:, None, :] * current
        hopped = dot(up_matrix, current_cut, (1, 0), high)
        applied = local_part + split_up(hopped, up_local, vec_local)
        following = advance(applied, current, previous, degree_step)
        if degree_step + 1 < DEGREE:
            applied_cut = split_down(local_part) + hopped
            following_cut = advance(applied_cut, current_cut, previous_cut, degree_step)
            previous_cut, current_cut = current_cut, following_cut
        previous, current = current, following
    row_panel = lax.all_to_all(current, "vec", split_axis=2, concat_axis=1, tiled=True)
    gram_sum = lax.psum(jnp.einsum("ukd,uld->kl", row_panel, row_panel, precision=highest), ("hil", "vec"))
    mixing = newton_schulz(gram_sum) * math.sqrt(up_matrix.shape[0] * down_count)
    row_panel = jnp.einsum("ukd,kl->uld", row_panel, mixing, precision=highest)
    return lax.all_to_all(row_panel, "vec", split_axis=1, concat_axis=2, tiled=True)


def on_device(start_block, down_matrix, hop_partner, hop_sign, bond_hop, onsite_u):
    hil_parts, vec_parts = lax.axis_size("hil"), lax.axis_size("vec")
    up_local, vec_local, _ = start_block.shape
    hop_coef = -bond_hop[:, None] * hop_sign.astype(jnp.float32)
    whole_vectors = vec_local % hil_parts == 0 and hil_parts % 8 == 0
    halved = vec_parts > 1 and vec_parts & (vec_parts - 1) == 0 and up_local % (16 * vec_parts) == 0
    plan = vector_cut if whole_vectors and halved else down_cut
    return plan(start_block, down_matrix, hop_coef, hop_partner, onsite_u)


def solution(mesh):
    in_specs = (P("hil", "vec", None), P(), P(), P(), P(), P())
    out_specs = P("hil", "vec", None)
    return jax.shard_map(
        on_device, mesh=mesh, in_specs=in_specs, out_specs=out_specs, check_vma=False
    )
```

```python
import functools
import math

import jax
import jax.numpy as jnp
from jax import lax
from jax.experimental import pallas as pl
from jax.experimental.pallas import tpu as pltpu
from jax.sharding import PartitionSpec as P

DEGREE = 2
NS_ITERS = 4
SUBLANES = 8
STACK = 4

highest = lax.Precision.HIGHEST
high = lax.Precision.HIGH
center_shift = 6.0
half_range = 12.0


def site_bits(states, sites):
    shifts = jnp.arange(sites, dtype=jnp.int32)
    return jnp.bitwise_and(jnp.right_shift(states[:, None], shifts[None, :]), 1).astype(jnp.float32)


def hop_matrix(hop_coef, hop_partner):
    up_count = hop_partner.shape[1]
    columns = jnp.arange(up_count, dtype=jnp.int32)
    total = jnp.zeros((up_count, up_count), jnp.float32)
    for bond in range(hop_partner.shape[0]):
        total = total + jnp.where(hop_partner[bond][:, None] == columns[None, :], hop_coef[bond][:, None], 0.0)
    return total


def dot(left, right, contract, precision):
    return lax.dot_general(
        left, right, ((contract[:1], contract[1:]), ((), ())), precision=precision, preferred_element_type=jnp.float32
    )


def apply_rows(vector, vector_rows, down_matrix, up_rows, diagonal_rows):
    applied = dot(vector_rows, down_matrix, (1, 1), high) + dot(up_rows, vector, (1, 0), high)
    return applied + diagonal_rows * vector_rows


def spread_step(held, step):
    pairs = [(i, i ^ step) for i in range(lax.axis_size("vec"))]
    return [lax.ppermute(piece, "vec", pairs) for piece in held]


def split(values):
    top = values.astype(jnp.bfloat16)
    return top, (values - top.astype(jnp.float32)).astype(jnp.bfloat16)


def vectors_first_kernel(place_ref, block_ref, out_ref):
    out_ref[...] = jnp.swapaxes(block_ref[...], 0, 1)


def vectors_first(start_block, turn, count, place):
    up_local, _, down_count = start_block.shape
    rows = min(32, up_local // 2)
    blocks = up_local // rows
    return pl.pallas_call(
        vectors_first_kernel,
        out_shape=jax.ShapeDtypeStruct((count, up_local, down_count), jnp.float32),
        grid_spec=pltpu.PrefetchScalarGridSpec(
            num_scalar_prefetch=1,
            grid=(blocks,),
            in_specs=[
                pl.BlockSpec(
                    (rows, count, down_count),
                    lambda i, place: (lax.rem(i + place[0] * (blocks // 2), blocks), turn, 0),
                )
            ],
            out_specs=pl.BlockSpec((count, rows, down_count), lambda i, place: (0, i, 0)),
        ),
        compiler_params=pltpu.CompilerParams(vmem_limit_bytes=56 * 1024 * 1024),
    )(place, start_block)


def joined(refs):
    return jnp.concatenate([ref[...] for ref in refs], axis=-1)


def grouped(refs, counts):
    ends = [sum(counts[: i + 1]) for i in range(len(counts))]
    return [refs[end - count : end] for end, count in zip(ends, counts)]


def stacked(refs, counts):
    return jnp.concatenate([jnp.swapaxes(joined(cuts), 0, 1) for cuts in grouped(refs, counts)], axis=1)


def gram_kernel(counts, start_ref, *refs):
    inputs, (top_ref, cross_ref) = refs[:-2], refs[-2:]

    @pl.when(pl.program_id(0) == 0)
    def _():
        top_ref[...] = jnp.zeros_like(top_ref)
        cross_ref[...] = jnp.zeros_like(cross_ref)

    values = stacked(inputs, counts)
    rows, vectors, columns = values.shape
    for first in range(0, rows, STACK):
        top, low = split(values[first : first + STACK].reshape(STACK * vectors, columns))
        top_ref[...] += dot(top, top, (1, 1), None)
        cross_ref[...] += dot(top, low, (1, 1), None)


def gram_partial(pieces, part, parts):
    vectors = sum(cuts[0].shape[0] for cuts in pieces)
    blocks = pieces[0][0].shape[1] // parts // SUBLANES
    flat = [cut for cuts in pieces for cut in cuts]
    specs = [
        pl.BlockSpec((cut.shape[0], SUBLANES, cut.shape[2]), lambda i, first: (0, first[0] + i, 0)) for cut in flat
    ]
    size = STACK * vectors
    out = jax.ShapeDtypeStruct((size, size), jnp.float32)
    top, cross = pl.pallas_call(
        functools.partial(gram_kernel, [len(cuts) for cuts in pieces]),
        out_shape=(out, out),
        grid_spec=pltpu.PrefetchScalarGridSpec(
            num_scalar_prefetch=1,
            grid=(blocks,),
            in_specs=specs,
            out_specs=[pl.BlockSpec((size, size), lambda i, first: (0, 0))] * 2,
        ),
        compiler_params=pltpu.CompilerParams(vmem_limit_bytes=48 * 1024 * 1024),
        cost_estimate=pl.CostEstimate(
            flops=4 * size * size * flat[0].shape[2] * blocks * SUBLANES // STACK,
            bytes_accessed=4 * sum(cut.size for cut in flat) // parts,
            transcendentals=0,
        ),
    )((part * blocks).reshape(1), *flat)
    cross = cross + cross.T
    total = (top + cross).reshape(STACK, vectors, STACK, vectors)
    return sum(total[u, :, u, :] for u in range(STACK))


def rotate_kernel(counts, place_ref, mix_ref, *refs):
    inputs, out_ref = refs[: sum(counts)], refs[-1]
    columns = out_ref.shape[2]
    mix_top, mix_low = split(mix_ref[...])
    count = mix_top.shape[0]
    both = jnp.concatenate([mix_top, mix_low], axis=0)
    top, low = split(jnp.concatenate([joined(cuts).reshape(-1, columns) for cuts in grouped(inputs, counts)], axis=0))
    wide = dot(both, top, (1, 0), None)
    result = wide[:count] + wide[count:] + dot(mix_top, low, (1, 0), None)
    out_ref[...] = result.reshape(SUBLANES, -1, columns)


def rotate_part(pieces, wide_mixing, place, half, segment, segments, earlier):
    half_rows = pieces[0][0].shape[1]
    down_count = pieces[0][0].shape[2]
    width = down_count // segments
    blocks = half_rows // SUBLANES
    own = wide_mixing.shape[0] // SUBLANES
    flat = [cut for cuts in pieces for cut in cuts]
    specs = [pl.BlockSpec(wide_mixing.shape, lambda i, place: (0, 0))]
    for cut in flat:
        column = segment if cut.shape[2] == down_count else 0
        shape = (cut.shape[0], SUBLANES, min(cut.shape[2], width))
        specs.append(pl.BlockSpec(shape, lambda i, place, column=column: (0, i, column)))
    operands = [place, wide_mixing, *flat]
    aliases = {}
    if earlier is not None:
        specs.append(pl.BlockSpec(memory_space=pl.ANY))
        aliases = {len(operands): 0}
        operands.append(earlier)
    return pl.pallas_call(
        functools.partial(rotate_kernel, [len(cuts) for cuts in pieces]),
        out_shape=jax.ShapeDtypeStruct((2 * half_rows, own, down_count), jnp.float32),
        grid_spec=pltpu.PrefetchScalarGridSpec(
            num_scalar_prefetch=1,
            grid=(blocks,),
            in_specs=specs,
            out_specs=pl.BlockSpec(
                (SUBLANES, own, width), lambda i, place: (i + lax.rem(place[0] + half, 2) * blocks, 0, segment)
            ),
        ),
        input_output_aliases=aliases,
        compiler_params=pltpu.CompilerParams(vmem_limit_bytes=56 * 1024 * 1024),
        cost_estimate=pl.CostEstimate(
            flops=6 * wide_mixing.size * width * blocks,
            bytes_accessed=4 * half_rows * width * (sum(cuts[0].shape[0] for cuts in pieces) + own),
            transcendentals=0,
        ),
    )(*operands)


def small_sum(values, axis):
    parts = lax.axis_size(axis)
    if parts & (parts - 1):
        return lax.psum(values, axis)
    step = 1
    while step < parts:
        count = min(4, parts // step)
        moved = []
        for distance in range(step, count * step, step):
            moved.append(lax.ppermute(values, axis, [(i, i ^ distance) for i in range(parts)]))
        for other in moved:
            values = values + other
        step *= count
    return values


def newton_schulz(gram_sum):
    identity = jnp.eye(gram_sum.shape[0], dtype=jnp.float32)
    norm_scale = 1.0 / jnp.sqrt(jnp.sqrt(jnp.sum(gram_sum * gram_sum)) + 1e-06)
    gram_sum = norm_scale * norm_scale * gram_sum
    product_total = identity
    for _ in range(NS_ITERS):
        mixing = 1.5 * identity - 0.5 * gram_sum
        product_total = dot(product_total, mixing, (1, 0), highest)
        gram_sum = dot(mixing, dot(gram_sum, mixing, (1, 0), highest), (1, 0), highest)
    return norm_scale * product_total


def vector_cut(start_block, down_matrix, hop_coef, hop_partner, onsite_u):
    hil_parts, vec_parts = lax.axis_size("hil"), lax.axis_size("vec")
    up_local, vec_local, down_count = start_block.shape
    up_count = up_local * hil_parts
    rounds = vec_local // hil_parts
    half_rows = up_local // 2
    side = vec_parts // 2
    own = lax.axis_index("vec")
    swap = own // side
    place = swap.reshape(1).astype(jnp.int32)

    def ordered(values):
        cut = values.reshape(values.shape[:-1] + (hil_parts, 2, half_rows))
        return jnp.where(swap == 1, cut[..., ::-1, :], cut).reshape(values.shape)

    arrived = []
    for turn in range(rounds):
        block = vectors_first(start_block, turn, hil_parts, place)
        block = lax.all_to_all(block, "hil", split_axis=0, concat_axis=0, tiled=True)
        arrived.append(block.reshape(up_count, down_count))
    other = jnp.where((hop_partner // half_rows) % 2 == 0, hop_partner + half_rows, hop_partner - half_rows)
    up_matrix = hop_matrix(ordered(hop_coef), ordered(jnp.where(swap == 1, other, hop_partner)))
    sites = onsite_u.shape[0]
    diagonal = -center_shift + jnp.dot(
        site_bits(ordered(jnp.arange(up_count, dtype=jnp.int32)), sites) * onsite_u[None, :],
        site_bits(jnp.arange(down_count, dtype=jnp.int32), sites).T,
        precision=highest,
        preferred_element_type=jnp.float32,
    )

    def rows(values, half):
        return values.reshape(hil_parts, 2, half_rows, -1)[:, half].reshape(hil_parts * half_rows, -1)

    def first_step(vector):
        return apply_rows(vector, vector, down_matrix, up_matrix, diagonal) / half_range

    def second_step(vector, before, half):
        applied = apply_rows(vector, rows(vector, half), down_matrix, rows(up_matrix, half), rows(diagonal, half))
        return (2.0 * applied / half_range - rows(before, half)).reshape(hil_parts, half_rows, down_count)

    mine, theirs = 0, 1
    once = first_step(arrived[0])
    pieces = [second_step(once, arrived[0], half) for half in (mine, theirs)]
    pieces[theirs], pieces[mine] = lax.optimization_barrier((pieces[theirs], pieces[mine]))
    crossed = []
    held = [[], []]
    for turn in range(rounds):
        upcoming = [None, None]
        for half in (theirs, mine):
            piece = pieces[half]
            if half == mine and turn + 1 < rounds:
                once = first_step(arrived[turn + 1])
                upcoming[theirs] = second_step(once, arrived[turn + 1], theirs)
                piece, once, upcoming[theirs] = lax.optimization_barrier((piece, once, upcoming[theirs]))
                upcoming[mine] = second_step(once, arrived[turn + 1], mine)
            if len(crossed) > 1:
                piece, crossed[-2] = lax.optimization_barrier((piece, crossed[-2]))
            back = lax.all_to_all(piece, "hil", split_axis=0, concat_axis=0, tiled=True)
            held[half].append(back)
            if (turn, half) == (rounds - 1, mine):
                bounds = [0, down_count // 4, down_count // 2, down_count]
                cuts = [back[:, :, begin:end] for begin, end in zip(bounds, bounds[1:])]
                crossed.append(spread_step(cuts[:1], side)[0])
            else:
                crossed.append(spread_step([back], side)[0])
        pieces = upcoming

    def on_side(near):
        step = side // 2
        while step >= 1:
            near = near + spread_step(near, step)
            step //= 2
        return near

    own_pieces = []
    for turn in range(rounds):
        own_pieces += [[piece] for piece in on_side([held[mine][turn]]) + on_side([crossed[2 * turn]])]
    step, distances = side // 2, [0]
    while step >= 1:
        distances += [distance ^ step for distance in distances]
        step //= 2
    distances += [distance ^ side for distance in distances]
    near = jnp.bitwise_xor(jnp.array(distances, dtype=jnp.int32), own)
    exchange = (near[:, None] == jnp.arange(vec_parts, dtype=jnp.int32)[None, :]).astype(jnp.float32)
    order = jnp.kron(jnp.eye(rounds, dtype=jnp.float32), jnp.kron(exchange, jnp.eye(hil_parts, dtype=jnp.float32)))
    order_own = order.reshape(rounds, vec_parts, hil_parts, -1)[:, 0].reshape(vec_local, -1)
    partial = gram_partial(own_pieces, lax.rem(own, side), side)
    partial = dot(order, dot(partial, order, (1, 0), highest), (0, 0), highest)
    partial, cuts[0] = lax.optimization_barrier((partial, crossed[-1]))
    partial, cuts[1] = lax.optimization_barrier((small_sum(partial, "vec"), cuts[1]))
    cuts[1] = spread_step(cuts[1:2], side)[0]
    gram_sum, cuts[1], cuts[2] = lax.optimization_barrier((small_sum(partial, "hil"), cuts[1], cuts[2]))
    cuts[2] = spread_step(cuts[2:], side)[0]
    mixing = newton_schulz(gram_sum) * math.sqrt(up_count * down_count)
    mixing = dot(dot(order_own, mixing, (1, 1), highest), order, (1, 1), highest)
    wide = jnp.arange(vec_local * SUBLANES, dtype=jnp.int32)
    long = jnp.arange(order.shape[0] * SUBLANES, dtype=jnp.int32)
    left = (wide[:, None] % vec_local == jnp.arange(vec_local, dtype=jnp.int32)[None, :]).astype(jnp.float32)
    right = (jnp.arange(order.shape[0], dtype=jnp.int32)[:, None] == long[None, :] // SUBLANES).astype(jnp.float32)
    wide_mixing = dot(left, dot(mixing, right, (1, 0), highest), (1, 0), highest)
    wide_mixing = jnp.where(wide[:, None] // vec_local == long[None, :] % SUBLANES, wide_mixing, 0.0)
    first = [list(pair) for pair in zip(on_side([cuts[0]]), on_side([cuts[1]]))]
    wide_mixing, first = lax.optimization_barrier((wide_mixing, first))
    result = rotate_part(own_pieces, wide_mixing, place, mine, 0, 1, None)
    here = [[piece] for turn in range(rounds) for piece in on_side([held[theirs][turn]])]
    there = [[piece] for turn in range(rounds - 1) for piece in on_side([crossed[2 * turn + 1]])]
    per_turn = len(first)
    columns = [there + first]
    result, cuts[2] = lax.optimization_barrier((result, cuts[2]))
    columns.append(there + [[piece] for piece in on_side([cuts[2]])])
    for segment, arrays in enumerate(columns):
        pieces = []
        for begin in range(0, rounds * per_turn, per_turn):
            pieces += here[begin : begin + per_turn] + arrays[begin : begin + per_turn]
        result = rotate_part(pieces, wide_mixing, place, theirs, segment, 2, result)
    return result


def split_down(local_block):
    hil_parts = lax.axis_size("hil")
    up_local, vec_local, down_count = local_block.shape
    down_local = down_count // hil_parts
    arranged = local_block.reshape(up_local, vec_local, hil_parts, down_local).transpose(2, 0, 1, 3)
    arranged = arranged.reshape(hil_parts, up_local, vec_local * down_local)
    received = lax.all_to_all(arranged, "hil", split_axis=0, concat_axis=1, tiled=True)
    return received.reshape(hil_parts * up_local, vec_local * down_local)


def split_up(spread, up_local, vec_local):
    hil_parts = lax.axis_size("hil")
    total_up, columns = spread.shape
    down_local = columns // vec_local
    received = lax.all_to_all(
        spread.reshape(1, total_up, columns), "hil", split_axis=1, concat_axis=0, tiled=True
    )
    arranged = received.reshape(hil_parts, up_local, vec_local, down_local).transpose(1, 2, 0, 3)
    return arranged.reshape(up_local, vec_local, hil_parts * down_local)


def advance(applied, present, earlier, degree_step):
    if degree_step == 0:
        return (applied - center_shift * present) / half_range
    return 2.0 * (applied - center_shift * present) / half_range - earlier


def down_cut(start_block, down_matrix, hop_coef, hop_partner, onsite_u):
    up_local, vec_local, down_count = start_block.shape
    up_matrix = hop_matrix(hop_coef, hop_partner)
    sites = onsite_u.shape[0]
    local_states = lax.axis_index("hil") * up_local + jnp.arange(up_local, dtype=jnp.int32)
    interaction = jnp.dot(
        site_bits(local_states, sites) * onsite_u[None, :],
        site_bits(jnp.arange(down_count, dtype=jnp.int32), sites).T,
        precision=highest,
        preferred_element_type=jnp.float32,
    )
    current = previous = start_block
    current_cut = previous_cut = split_down(current)
    for degree_step in range(DEGREE):
        local_part = dot(current.reshape(up_local * vec_local, down_count), down_matrix, (1, 1), high)
        local_part = local_part.reshape(current.shape) + interaction[:, None, :] * current
        hopped = dot(up_matrix, current_cut, (1, 0), high)
        applied = local_part + split_up(hopped, up_local, vec_local)
        following = advance(applied, current, previous, degree_step)
        if degree_step + 1 < DEGREE:
            applied_cut = split_down(local_part) + hopped
            following_cut = advance(applied_cut, current_cut, previous_cut, degree_step)
            previous_cut, current_cut = current_cut, following_cut
        previous, current = current, following
    row_panel = lax.all_to_all(current, "vec", split_axis=2, concat_axis=1, tiled=True)
    gram_sum = lax.psum(jnp.einsum("ukd,uld->kl", row_panel, row_panel, precision=highest), ("hil", "vec"))
    mixing = newton_schulz(gram_sum) * math.sqrt(up_matrix.shape[0] * down_count)
    row_panel = jnp.einsum("ukd,kl->uld", row_panel, mixing, precision=highest)
    return lax.all_to_all(row_panel, "vec", split_axis=1, concat_axis=2, tiled=True)


def on_device(start_block, down_matrix, hop_partner, hop_sign, bond_hop, onsite_u):
    hil_parts, vec_parts = lax.axis_size("hil"), lax.axis_size("vec")
    up_local, vec_local, _ = start_block.shape
    hop_coef = -bond_hop[:, None] * hop_sign.astype(jnp.float32)
    whole_vectors = vec_local % hil_parts == 0 and hil_parts % 8 == 0
    halved = vec_parts > 1 and vec_parts & (vec_parts - 1) == 0 and up_local % (16 * vec_parts) == 0
    plan = vector_cut if whole_vectors and halved else down_cut
    return plan(start_block, down_matrix, hop_coef, hop_partner, onsite_u)


def solution(mesh):
    in_specs = (P("hil", "vec", None), P(), P(), P(), P(), P())
    out_specs = P("hil", "vec", None)
    return jax.shard_map(
        on_device, mesh=mesh, in_specs=in_specs, out_specs=out_specs, check_vma=False
    )
```

```python
import functools
import math

import jax
import jax.numpy as jnp
from jax import lax
from jax.experimental import pallas as pl
from jax.experimental.pallas import tpu as pltpu
from jax.sharding import PartitionSpec as P

DEGREE = 2
NS_ITERS = 4
SUBLANES = 8
STACK = 4

highest = lax.Precision.HIGHEST
high = lax.Precision.HIGH
center_shift = 6.0
half_range = 12.0


def site_bits(states, sites):
    shifts = jnp.arange(sites, dtype=jnp.int32)
    return jnp.bitwise_and(jnp.right_shift(states[:, None], shifts[None, :]), 1).astype(jnp.float32)


def hop_matrix(hop_coef, hop_partner):
    up_count = hop_partner.shape[1]
    columns = jnp.arange(up_count, dtype=jnp.int32)
    total = jnp.zeros((up_count, up_count), jnp.float32)
    for bond in range(hop_partner.shape[0]):
        total = total + jnp.where(hop_partner[bond][:, None] == columns[None, :], hop_coef[bond][:, None], 0.0)
    return total


def dot(left, right, contract, precision):
    return lax.dot_general(
        left, right, ((contract[:1], contract[1:]), ((), ())), precision=precision, preferred_element_type=jnp.float32
    )


def apply_rows(vector, vector_rows, down_matrix, up_rows, diagonal_rows):
    applied = dot(vector_rows, down_matrix, (1, 1), high) + dot(up_rows, vector, (1, 0), high)
    return applied + diagonal_rows * vector_rows


def spread_step(held, step):
    pairs = [(i, i ^ step) for i in range(lax.axis_size("vec"))]
    return [lax.ppermute(piece, "vec", pairs) for piece in held]


def split(values):
    top = values.astype(jnp.bfloat16)
    return top, (values - top.astype(jnp.float32)).astype(jnp.bfloat16)


def vectors_first_kernel(place_ref, block_ref, out_ref):
    out_ref[...] = jnp.swapaxes(block_ref[...], 0, 1)


def vectors_first(start_block, turn, count, place):
    up_local, _, down_count = start_block.shape
    rows = min(32, up_local // 2)
    blocks = up_local // rows
    return pl.pallas_call(
        vectors_first_kernel,
        out_shape=jax.ShapeDtypeStruct((count, up_local, down_count), jnp.float32),
        grid_spec=pltpu.PrefetchScalarGridSpec(
            num_scalar_prefetch=1,
            grid=(blocks,),
            in_specs=[
                pl.BlockSpec(
                    (rows, count, down_count),
                    lambda i, place: (lax.rem(i + place[0] * (blocks // 2), blocks), turn, 0),
                )
            ],
            out_specs=pl.BlockSpec((count, rows, down_count), lambda i, place: (0, i, 0)),
        ),
        compiler_params=pltpu.CompilerParams(vmem_limit_bytes=56 * 1024 * 1024),
    )(place, start_block)


def joined(refs):
    return jnp.concatenate([ref[...] for ref in refs], axis=-1)


def grouped(refs, counts):
    ends = [sum(counts[: i + 1]) for i in range(len(counts))]
    return [refs[end - count : end] for end, count in zip(ends, counts)]


def stacked(refs, counts):
    return jnp.concatenate([jnp.swapaxes(joined(cuts), 0, 1) for cuts in grouped(refs, counts)], axis=1)


def gram_kernel(counts, start_ref, *refs):
    inputs, (top_ref, cross_ref) = refs[:-2], refs[-2:]

    @pl.when(pl.program_id(0) == 0)
    def _():
        top_ref[...] = jnp.zeros_like(top_ref)
        cross_ref[...] = jnp.zeros_like(cross_ref)

    values = stacked(inputs, counts)
    rows, vectors, columns = values.shape
    for first in range(0, rows, STACK):
        top, low = split(values[first : first + STACK].reshape(STACK * vectors, columns))
        top_ref[...] += dot(top, top, (1, 1), None)
        cross_ref[...] += dot(top, low, (1, 1), None)


def gram_partial(pieces, part, parts):
    vectors = sum(cuts[0].shape[0] for cuts in pieces)
    blocks = pieces[0][0].shape[1] // parts // SUBLANES
    flat = [cut for cuts in pieces for cut in cuts]
    specs = [
        pl.BlockSpec((cut.shape[0], SUBLANES, cut.shape[2]), lambda i, first: (0, first[0] + i, 0)) for cut in flat
    ]
    size = STACK * vectors
    out = jax.ShapeDtypeStruct((size, size), jnp.float32)
    top, cross = pl.pallas_call(
        functools.partial(gram_kernel, [len(cuts) for cuts in pieces]),
        out_shape=(out, out),
        grid_spec=pltpu.PrefetchScalarGridSpec(
            num_scalar_prefetch=1,
            grid=(blocks,),
            in_specs=specs,
            out_specs=[pl.BlockSpec((size, size), lambda i, first: (0, 0))] * 2,
        ),
        compiler_params=pltpu.CompilerParams(vmem_limit_bytes=48 * 1024 * 1024),
        cost_estimate=pl.CostEstimate(
            flops=4 * size * size * flat[0].shape[2] * blocks * SUBLANES // STACK,
            bytes_accessed=4 * sum(cut.size for cut in flat) // parts,
            transcendentals=0,
        ),
    )((part * blocks).reshape(1), *flat)
    cross = cross + cross.T
    total = (top + cross).reshape(STACK, vectors, STACK, vectors)
    return sum(total[u, :, u, :] for u in range(STACK))


def rotate_kernel(counts, place_ref, mix_ref, *refs):
    inputs, out_ref, both_ref = refs[: sum(counts)], refs[-2], refs[-1]
    rows, _, columns = out_ref.shape
    count = mix_ref.shape[0]

    @pl.when(pl.program_id(0) == 0)
    def _():
        mix_top, mix_low = split(mix_ref[...])
        both_ref[:count] = mix_top
        both_ref[count:] = mix_low

    for first in range(0, rows, SUBLANES):
        blocks = []
        for cuts in grouped(inputs, counts):
            block = jnp.concatenate([ref[:, first : first + SUBLANES, :] for ref in cuts], axis=-1)
            blocks.append(block.reshape(-1, columns))
        top, low = split(jnp.concatenate(blocks, axis=0))
        wide = dot(both_ref[...], top, (1, 0), None)
        result = wide[:count] + wide[count:] + dot(both_ref[:count], low, (1, 0), None)
        out_ref[first : first + SUBLANES] = result.reshape(SUBLANES, -1, columns)


def rotate_half(pieces, wide_mixing, place, half, earlier):
    half_rows = pieces[0][0].shape[1]
    down_count = sum(cut.shape[2] for cut in pieces[0])
    step_rows = 2 * SUBLANES
    blocks = half_rows // step_rows
    own = wide_mixing.shape[0] // SUBLANES
    flat = [cut for cuts in pieces for cut in cuts]
    specs = [pl.BlockSpec(wide_mixing.shape, lambda i, place: (0, 0))]
    for cut in flat:
        specs.append(pl.BlockSpec((cut.shape[0], step_rows, cut.shape[2]), lambda i, place: (0, i, 0)))
    operands = [place, wide_mixing, *flat]
    aliases = {}
    if earlier is not None:
        specs.append(pl.BlockSpec(memory_space=pl.ANY))
        aliases = {len(operands): 0}
        operands.append(earlier)
    return pl.pallas_call(
        functools.partial(rotate_kernel, [len(cuts) for cuts in pieces]),
        out_shape=jax.ShapeDtypeStruct((2 * half_rows, own, down_count), jnp.float32),
        grid_spec=pltpu.PrefetchScalarGridSpec(
            num_scalar_prefetch=1,
            grid=(blocks,),
            in_specs=specs,
            out_specs=pl.BlockSpec(
                (step_rows, own, down_count), lambda i, place: (i + lax.rem(place[0] + half, 2) * blocks, 0, 0)
            ),
            scratch_shapes=[pltpu.VMEM((2 * wide_mixing.shape[0], wide_mixing.shape[1]), jnp.bfloat16)],
        ),
        input_output_aliases=aliases,
        compiler_params=pltpu.CompilerParams(vmem_limit_bytes=56 * 1024 * 1024),
        cost_estimate=pl.CostEstimate(
            flops=6 * wide_mixing.size * down_count * half_rows // SUBLANES,
            bytes_accessed=4 * (sum(cut.size for cut in flat) + half_rows * own * down_count),
            transcendentals=0,
        ),
    )(*operands)


def small_sum(values, axis):
    parts = lax.axis_size(axis)
    if parts & (parts - 1):
        return lax.psum(values, axis)
    step = 1
    while step < parts:
        count = min(4, parts // step)
        moved = []
        for distance in range(step, count * step, step):
            moved.append(lax.ppermute(values, axis, [(i, i ^ distance) for i in range(parts)]))
        for other in moved:
            values = values + other
        step *= count
    return values


def newton_schulz(gram_sum):
    identity = jnp.eye(gram_sum.shape[0], dtype=jnp.float32)
    norm_scale = 1.0 / jnp.sqrt(jnp.sqrt(jnp.sum(gram_sum * gram_sum)) + 1e-06)
    gram_sum = norm_scale * norm_scale * gram_sum
    product_total = identity
    for _ in range(NS_ITERS):
        mixing = 1.5 * identity - 0.5 * gram_sum
        product_total = dot(product_total, mixing, (1, 0), highest)
        gram_sum = dot(mixing, dot(gram_sum, mixing, (1, 0), highest), (1, 0), highest)
    return norm_scale * product_total


def vector_cut(start_block, down_matrix, hop_coef, hop_partner, onsite_u):
    hil_parts, vec_parts = lax.axis_size("hil"), lax.axis_size("vec")
    up_local, vec_local, down_count = start_block.shape
    up_count = up_local * hil_parts
    rounds = vec_local // hil_parts
    half_rows = up_local // 2
    side = vec_parts // 2
    own = lax.axis_index("vec")
    swap = own // side
    place = swap.reshape(1).astype(jnp.int32)

    def ordered(values):
        cut = values.reshape(values.shape[:-1] + (hil_parts, 2, half_rows))
        return jnp.where(swap == 1, cut[..., ::-1, :], cut).reshape(values.shape)

    arrived = []
    for turn in range(rounds):
        block = vectors_first(start_block, turn, hil_parts, place)
        block = lax.all_to_all(block, "hil", split_axis=0, concat_axis=0, tiled=True)
        arrived.append(block.reshape(up_count, down_count))
    other = jnp.where((hop_partner // half_rows) % 2 == 0, hop_partner + half_rows, hop_partner - half_rows)
    up_matrix = hop_matrix(ordered(hop_coef), ordered(jnp.where(swap == 1, other, hop_partner)))
    sites = onsite_u.shape[0]
    diagonal = -center_shift + jnp.dot(
        site_bits(ordered(jnp.arange(up_count, dtype=jnp.int32)), sites) * onsite_u[None, :],
        site_bits(jnp.arange(down_count, dtype=jnp.int32), sites).T,
        precision=highest,
        preferred_element_type=jnp.float32,
    )

    def rows(values, half):
        return values.reshape(hil_parts, 2, half_rows, -1)[:, half].reshape(hil_parts * half_rows, -1)

    def first_step(vector):
        return apply_rows(vector, vector, down_matrix, up_matrix, diagonal) / half_range

    def second_step(vector, before, half):
        applied = apply_rows(vector, rows(vector, half), down_matrix, rows(up_matrix, half), rows(diagonal, half))
        return (2.0 * applied / half_range - rows(before, half)).reshape(hil_parts, half_rows, down_count)

    mine, theirs = 0, 1
    once = first_step(arrived[0])
    pieces = [second_step(once, arrived[0], half) for half in (mine, theirs)]
    pieces[theirs], pieces[mine] = lax.optimization_barrier((pieces[theirs], pieces[mine]))
    crossed = []
    held = [[], []]
    for turn in range(rounds):
        upcoming = [None, None]
        for half in (theirs, mine):
            piece = pieces[half]
            if half == mine and turn + 1 < rounds:
                once = first_step(arrived[turn + 1])
                upcoming[theirs] = second_step(once, arrived[turn + 1], theirs)
                piece, once, upcoming[theirs] = lax.optimization_barrier((piece, once, upcoming[theirs]))
                upcoming[mine] = second_step(once, arrived[turn + 1], mine)
            if len(crossed) > 1:
                piece, crossed[-2] = lax.optimization_barrier((piece, crossed[-2]))
            back = lax.all_to_all(piece, "hil", split_axis=0, concat_axis=0, tiled=True)
            held[half].append(back)
            if (turn, half) == (rounds - 1, mine):
                bounds = [0, down_count // 8 * 3, down_count // 8 * 5, down_count]
                cuts = [back[:, :, begin:end] for begin, end in zip(bounds, bounds[1:])]
                crossed.append(spread_step(cuts[:1], side)[0])
            else:
                crossed.append(spread_step([back], side)[0])
        pieces = upcoming

    def on_side(near):
        step = side // 2
        while step >= 1:
            near = near + spread_step(near, step)
            step //= 2
        return near

    own_pieces = []
    for turn in range(rounds):
        own_pieces += [[piece] for piece in on_side([held[mine][turn]]) + on_side([crossed[2 * turn]])]
    step, distances = side // 2, [0]
    while step >= 1:
        distances += [distance ^ step for distance in distances]
        step //= 2
    distances += [distance ^ side for distance in distances]
    near = jnp.bitwise_xor(jnp.array(distances, dtype=jnp.int32), own)
    exchange = (near[:, None] == jnp.arange(vec_parts, dtype=jnp.int32)[None, :]).astype(jnp.float32)
    order = jnp.kron(jnp.eye(rounds, dtype=jnp.float32), jnp.kron(exchange, jnp.eye(hil_parts, dtype=jnp.float32)))
    order_own = order.reshape(rounds, vec_parts, hil_parts, -1)[:, 0].reshape(vec_local, -1)
    partial = gram_partial(own_pieces, lax.rem(own, side), side)
    partial = dot(order, dot(partial, order, (1, 0), highest), (0, 0), highest)
    partial, cuts[0] = lax.optimization_barrier((partial, crossed[-1]))
    partial, cuts[1], cuts[2] = lax.optimization_barrier((small_sum(partial, "vec"), cuts[1], cuts[2]))
    cuts[1:] = spread_step(cuts[1:], side)
    gram_sum, cuts[1] = lax.optimization_barrier((small_sum(partial, "hil"), cuts[1]))
    mixing = newton_schulz(gram_sum) * math.sqrt(up_count * down_count)
    mixing = dot(dot(order_own, mixing, (1, 1), highest), order, (1, 1), highest)
    wide = jnp.arange(vec_local * SUBLANES, dtype=jnp.int32)
    long = jnp.arange(order.shape[0] * SUBLANES, dtype=jnp.int32)
    left = (wide[:, None] % vec_local == jnp.arange(vec_local, dtype=jnp.int32)[None, :]).astype(jnp.float32)
    right = (jnp.arange(order.shape[0], dtype=jnp.int32)[:, None] == long[None, :] // SUBLANES).astype(jnp.float32)
    wide_mixing = dot(left, dot(mixing, right, (1, 0), highest), (1, 0), highest)
    wide_mixing = jnp.where(wide[:, None] // vec_local == long[None, :] % SUBLANES, wide_mixing, 0.0)
    result = rotate_half(own_pieces, wide_mixing, place, mine, None)
    result, cuts[2] = lax.optimization_barrier((result, cuts[2]))
    other_pieces = []
    for turn in range(rounds):
        there = cuts if turn == rounds - 1 else [crossed[2 * turn + 1]]
        here = [[piece] for piece in on_side([held[theirs][turn]])]
        there = [list(group) for group in zip(*[on_side([cut]) for cut in there])]
        other_pieces += here + there
    return rotate_half(other_pieces, wide_mixing, place, theirs, result)


def split_down(local_block):
    hil_parts = lax.axis_size("hil")
    up_local, vec_local, down_count = local_block.shape
    down_local = down_count // hil_parts
    arranged = local_block.reshape(up_local, vec_local, hil_parts, down_local).transpose(2, 0, 1, 3)
    arranged = arranged.reshape(hil_parts, up_local, vec_local * down_local)
    received = lax.all_to_all(arranged, "hil", split_axis=0, concat_axis=1, tiled=True)
    return received.reshape(hil_parts * up_local, vec_local * down_local)


def split_up(spread, up_local, vec_local):
    hil_parts = lax.axis_size("hil")
    total_up, columns = spread.shape
    down_local = columns // vec_local
    received = lax.all_to_all(
        spread.reshape(1, total_up, columns), "hil", split_axis=1, concat_axis=0, tiled=True
    )
    arranged = received.reshape(hil_parts, up_local, vec_local, down_local).transpose(1, 2, 0, 3)
    return arranged.reshape(up_local, vec_local, hil_parts * down_local)


def advance(applied, present, earlier, degree_step):
    if degree_step == 0:
        return (applied - center_shift * present) / half_range
    return 2.0 * (applied - center_shift * present) / half_range - earlier


def down_cut(start_block, down_matrix, hop_coef, hop_partner, onsite_u):
    up_local, vec_local, down_count = start_block.shape
    up_matrix = hop_matrix(hop_coef, hop_partner)
    sites = onsite_u.shape[0]
    local_states = lax.axis_index("hil") * up_local + jnp.arange(up_local, dtype=jnp.int32)
    interaction = jnp.dot(
        site_bits(local_states, sites) * onsite_u[None, :],
        site_bits(jnp.arange(down_count, dtype=jnp.int32), sites).T,
        precision=highest,
        preferred_element_type=jnp.float32,
    )
    current = previous = start_block
    current_cut = previous_cut = split_down(current)
    for degree_step in range(DEGREE):
        local_part = dot(current.reshape(up_local * vec_local, down_count), down_matrix, (1, 1), high)
        local_part = local_part.reshape(current.shape) + interaction[:, None, :] * current
        hopped = dot(up_matrix, current_cut, (1, 0), high)
        applied = local_part + split_up(hopped, up_local, vec_local)
        following = advance(applied, current, previous, degree_step)
        if degree_step + 1 < DEGREE:
            applied_cut = split_down(local_part) + hopped
            following_cut = advance(applied_cut, current_cut, previous_cut, degree_step)
            previous_cut, current_cut = current_cut, following_cut
        previous, current = current, following
    row_panel = lax.all_to_all(current, "vec", split_axis=2, concat_axis=1, tiled=True)
    gram_sum = lax.psum(jnp.einsum("ukd,uld->kl", row_panel, row_panel, precision=highest), ("hil", "vec"))
    mixing = newton_schulz(gram_sum) * math.sqrt(up_matrix.shape[0] * down_count)
    row_panel = jnp.einsum("ukd,kl->uld", row_panel, mixing, precision=highest)
    return lax.all_to_all(row_panel, "vec", split_axis=1, concat_axis=2, tiled=True)


def on_device(start_block, down_matrix, hop_partner, hop_sign, bond_hop, onsite_u):
    hil_parts, vec_parts = lax.axis_size("hil"), lax.axis_size("vec")
    up_local, vec_local, _ = start_block.shape
    hop_coef = -bond_hop[:, None] * hop_sign.astype(jnp.float32)
    whole_vectors = vec_local % hil_parts == 0 and hil_parts % 8 == 0
    halved = vec_parts > 1 and vec_parts & (vec_parts - 1) == 0 and up_local % (16 * vec_parts) == 0
    plan = vector_cut if whole_vectors and halved else down_cut
    return plan(start_block, down_matrix, hop_coef, hop_partner, onsite_u)


def solution(mesh):
    in_specs = (P("hil", "vec", None), P(), P(), P(), P(), P())
    out_specs = P("hil", "vec", None)
    return jax.shard_map(
        on_device, mesh=mesh, in_specs=in_specs, out_specs=out_specs, check_vma=False
    )
```

```python
import functools
import math

import jax
import jax.numpy as jnp
from jax import lax
from jax.experimental import pallas as pl
from jax.experimental.pallas import tpu as pltpu
from jax.sharding import PartitionSpec as P

DEGREE = 2
NS_ITERS = 4
SUBLANES = 8
STACK = 4

highest = lax.Precision.HIGHEST
high = lax.Precision.HIGH
center_shift = 6.0
half_range = 12.0


def site_bits(states, sites):
    shifts = jnp.arange(sites, dtype=jnp.int32)
    return jnp.bitwise_and(jnp.right_shift(states[:, None], shifts[None, :]), 1).astype(jnp.float32)


def hop_matrix(hop_coef, hop_partner):
    up_count = hop_partner.shape[1]
    columns = jnp.arange(up_count, dtype=jnp.int32)
    total = jnp.zeros((up_count, up_count), jnp.float32)
    for bond in range(hop_partner.shape[0]):
        total = total + jnp.where(hop_partner[bond][:, None] == columns[None, :], hop_coef[bond][:, None], 0.0)
    return total


def dot(left, right, contract, precision):
    return lax.dot_general(
        left, right, ((contract[:1], contract[1:]), ((), ())), precision=precision, preferred_element_type=jnp.float32
    )


def apply_rows(vector, vector_rows, down_matrix, up_rows, diagonal_rows):
    applied = dot(vector_rows, down_matrix, (1, 1), high) + dot(up_rows, vector, (1, 0), high)
    return applied + diagonal_rows * vector_rows


def spread_step(held, step):
    pairs = [(i, i ^ step) for i in range(lax.axis_size("vec"))]
    return [lax.ppermute(piece, "vec", pairs) for piece in held]


def split(values):
    top = values.astype(jnp.bfloat16)
    return top, (values - top.astype(jnp.float32)).astype(jnp.bfloat16)


def vectors_first_kernel(place_ref, block_ref, out_ref):
    out_ref[...] = jnp.swapaxes(block_ref[...], 0, 1)


def vectors_first(start_block, turn, count, place):
    up_local, _, down_count = start_block.shape
    rows = min(32, up_local // 2)
    blocks = up_local // rows
    return pl.pallas_call(
        vectors_first_kernel,
        out_shape=jax.ShapeDtypeStruct((count, up_local, down_count), jnp.float32),
        grid_spec=pltpu.PrefetchScalarGridSpec(
            num_scalar_prefetch=1,
            grid=(blocks,),
            in_specs=[
                pl.BlockSpec(
                    (rows, count, down_count),
                    lambda i, place: (lax.rem(i + place[0] * (blocks // 2), blocks), turn, 0),
                )
            ],
            out_specs=pl.BlockSpec((count, rows, down_count), lambda i, place: (0, i, 0)),
        ),
        compiler_params=pltpu.CompilerParams(vmem_limit_bytes=56 * 1024 * 1024),
    )(place, start_block)


def joined(refs):
    return jnp.concatenate([ref[...] for ref in refs], axis=-1)


def grouped(refs, counts):
    ends = [sum(counts[: i + 1]) for i in range(len(counts))]
    return [refs[end - count : end] for end, count in zip(ends, counts)]


def stacked(refs, counts):
    return jnp.concatenate([jnp.swapaxes(joined(cuts), 0, 1) for cuts in grouped(refs, counts)], axis=1)


def gram_kernel(counts, start_ref, *refs):
    inputs, (top_ref, cross_ref) = refs[:-2], refs[-2:]

    @pl.when(pl.program_id(0) == 0)
    def _():
        top_ref[...] = jnp.zeros_like(top_ref)
        cross_ref[...] = jnp.zeros_like(cross_ref)

    values = stacked(inputs, counts)
    rows, vectors, columns = values.shape
    for first in range(0, rows, STACK):
        top, low = split(values[first : first + STACK].reshape(STACK * vectors, columns))
        top_ref[...] += dot(top, top, (1, 1), None)
        cross_ref[...] += dot(top, low, (1, 1), None)


def gram_partial(pieces, part, parts):
    vectors = sum(cuts[0].shape[0] for cuts in pieces)
    blocks = pieces[0][0].shape[1] // parts // SUBLANES
    flat = [cut for cuts in pieces for cut in cuts]
    specs = [
        pl.BlockSpec((cut.shape[0], SUBLANES, cut.shape[2]), lambda i, first: (0, first[0] + i, 0)) for cut in flat
    ]
    size = STACK * vectors
    out = jax.ShapeDtypeStruct((size, size), jnp.float32)
    top, cross = pl.pallas_call(
        functools.partial(gram_kernel, [len(cuts) for cuts in pieces]),
        out_shape=(out, out),
        grid_spec=pltpu.PrefetchScalarGridSpec(
            num_scalar_prefetch=1,
            grid=(blocks,),
            in_specs=specs,
            out_specs=[pl.BlockSpec((size, size), lambda i, first: (0, 0))] * 2,
        ),
        compiler_params=pltpu.CompilerParams(vmem_limit_bytes=48 * 1024 * 1024),
        cost_estimate=pl.CostEstimate(
            flops=4 * size * size * flat[0].shape[2] * blocks * SUBLANES // STACK,
            bytes_accessed=4 * sum(cut.size for cut in flat) // parts,
            transcendentals=0,
        ),
    )((part * blocks).reshape(1), *flat)
    cross = cross + cross.T
    total = (top + cross).reshape(STACK, vectors, STACK, vectors)
    return sum(total[u, :, u, :] for u in range(STACK))


def rotate_kernel(counts, place_ref, mix_ref, *refs):
    inputs, out_ref, both_ref = refs[: sum(counts)], refs[-2], refs[-1]
    rows, _, columns = out_ref.shape
    count = mix_ref.shape[0]

    @pl.when(pl.program_id(0) == 0)
    def _():
        mix_top, mix_low = split(mix_ref[...])
        both_ref[:count] = mix_top
        both_ref[count:] = mix_low

    for first in range(0, rows, SUBLANES):
        blocks = []
        for cuts in grouped(inputs, counts):
            block = jnp.concatenate([ref[:, first : first + SUBLANES, :] for ref in cuts], axis=-1)
            blocks.append(block.reshape(-1, columns))
        top, low = split(jnp.concatenate(blocks, axis=0))
        wide = dot(both_ref[...], top, (1, 0), None)
        result = wide[:count] + wide[count:] + dot(both_ref[:count], low, (1, 0), None)
        out_ref[first : first + SUBLANES] = result.reshape(SUBLANES, -1, columns)


def rotate_part(pieces, wide_mixing, place, half, column, width, earlier):
    half_rows = pieces[0][0].shape[1]
    down_count = pieces[0][0].shape[2]
    step_rows = 2 * SUBLANES
    blocks = half_rows // step_rows
    own = wide_mixing.shape[0] // SUBLANES
    flat = [cut for cuts in pieces for cut in cuts]
    specs = [pl.BlockSpec(wide_mixing.shape, lambda i, place: (0, 0))]
    for cut in flat:
        shape = (cut.shape[0], step_rows, min(cut.shape[2], width))
        specs.append(pl.BlockSpec(shape, lambda i, place, at=column if cut.shape[2] == down_count else 0: (0, i, at)))
    operands = [place, wide_mixing, *flat]
    aliases = {}
    if earlier is not None:
        specs.append(pl.BlockSpec(memory_space=pl.ANY))
        aliases = {len(operands): 0}
        operands.append(earlier)
    return pl.pallas_call(
        functools.partial(rotate_kernel, [len(cuts) for cuts in pieces]),
        out_shape=jax.ShapeDtypeStruct((2 * half_rows, own, down_count), jnp.float32),
        grid_spec=pltpu.PrefetchScalarGridSpec(
            num_scalar_prefetch=1,
            grid=(blocks,),
            in_specs=specs,
            out_specs=pl.BlockSpec(
                (step_rows, own, width), lambda i, place: (i + lax.rem(place[0] + half, 2) * blocks, 0, column)
            ),
            scratch_shapes=[pltpu.VMEM((2 * wide_mixing.shape[0], wide_mixing.shape[1]), jnp.bfloat16)],
        ),
        input_output_aliases=aliases,
        compiler_params=pltpu.CompilerParams(vmem_limit_bytes=56 * 1024 * 1024),
        cost_estimate=pl.CostEstimate(
            flops=6 * wide_mixing.size * width * half_rows // SUBLANES,
            bytes_accessed=4 * half_rows * width * (sum(cuts[0].shape[0] for cuts in pieces) + own),
            transcendentals=0,
        ),
    )(*operands)


def small_sum(values, axis):
    parts = lax.axis_size(axis)
    if parts & (parts - 1):
        return lax.psum(values, axis)
    step = 1
    while step < parts:
        count = min(4, parts // step)
        moved = []
        for distance in range(step, count * step, step):
            moved.append(lax.ppermute(values, axis, [(i, i ^ distance) for i in range(parts)]))
        for other in moved:
            values = values + other
        step *= count
    return values


def newton_schulz(gram_sum):
    identity = jnp.eye(gram_sum.shape[0], dtype=jnp.float32)
    norm_scale = 1.0 / jnp.sqrt(jnp.sqrt(jnp.sum(gram_sum * gram_sum)) + 1e-06)
    gram_sum = norm_scale * norm_scale * gram_sum
    product_total = identity
    for _ in range(NS_ITERS):
        mixing = 1.5 * identity - 0.5 * gram_sum
        product_total = dot(product_total, mixing, (1, 0), highest)
        gram_sum = dot(mixing, dot(gram_sum, mixing, (1, 0), highest), (1, 0), highest)
    return norm_scale * product_total


def vector_cut(start_block, down_matrix, hop_coef, hop_partner, onsite_u):
    hil_parts, vec_parts = lax.axis_size("hil"), lax.axis_size("vec")
    up_local, vec_local, down_count = start_block.shape
    up_count = up_local * hil_parts
    rounds = vec_local // hil_parts
    half_rows = up_local // 2
    side = vec_parts // 2
    own = lax.axis_index("vec")
    swap = own // side
    place = swap.reshape(1).astype(jnp.int32)

    def ordered(values):
        cut = values.reshape(values.shape[:-1] + (hil_parts, 2, half_rows))
        return jnp.where(swap == 1, cut[..., ::-1, :], cut).reshape(values.shape)

    arrived = []
    for turn in range(rounds):
        block = vectors_first(start_block, turn, hil_parts, place)
        block = lax.all_to_all(block, "hil", split_axis=0, concat_axis=0, tiled=True)
        arrived.append(block.reshape(up_count, down_count))
    other = jnp.where((hop_partner // half_rows) % 2 == 0, hop_partner + half_rows, hop_partner - half_rows)
    up_matrix = hop_matrix(ordered(hop_coef), ordered(jnp.where(swap == 1, other, hop_partner)))
    sites = onsite_u.shape[0]
    diagonal = -center_shift + jnp.dot(
        site_bits(ordered(jnp.arange(up_count, dtype=jnp.int32)), sites) * onsite_u[None, :],
        site_bits(jnp.arange(down_count, dtype=jnp.int32), sites).T,
        precision=highest,
        preferred_element_type=jnp.float32,
    )

    def rows(values, half):
        return values.reshape(hil_parts, 2, half_rows, -1)[:, half].reshape(hil_parts * half_rows, -1)

    def first_step(vector):
        return apply_rows(vector, vector, down_matrix, up_matrix, diagonal) / half_range

    def second_step(vector, before, half):
        applied = apply_rows(vector, rows(vector, half), down_matrix, rows(up_matrix, half), rows(diagonal, half))
        return (2.0 * applied / half_range - rows(before, half)).reshape(hil_parts, half_rows, down_count)

    mine, theirs = 0, 1
    once = first_step(arrived[0])
    pieces = [second_step(once, arrived[0], half) for half in (mine, theirs)]
    pieces[theirs], pieces[mine] = lax.optimization_barrier((pieces[theirs], pieces[mine]))
    crossed = []
    held = [[], []]
    for turn in range(rounds):
        upcoming = [None, None]
        for half in (theirs, mine):
            piece = pieces[half]
            if half == mine and turn + 1 < rounds:
                once = first_step(arrived[turn + 1])
                upcoming[theirs] = second_step(once, arrived[turn + 1], theirs)
                piece, once, upcoming[theirs] = lax.optimization_barrier((piece, once, upcoming[theirs]))
                upcoming[mine] = second_step(once, arrived[turn + 1], mine)
            if len(crossed) > 1:
                piece, crossed[-2] = lax.optimization_barrier((piece, crossed[-2]))
            back = lax.all_to_all(piece, "hil", split_axis=0, concat_axis=0, tiled=True)
            held[half].append(back)
            if (turn, half) == (rounds - 1, mine):
                bounds = [down_count // 4 * number for number in range(5)]
                crossed.append(spread_step([back[:, :, : bounds[1]]], side)[0])
            else:
                crossed.append(spread_step([back], side)[0])
        pieces = upcoming

    def on_side(near):
        step = side // 2
        while step >= 1:
            near = near + spread_step(near, step)
            step //= 2
        return near

    own_pieces = []
    for turn in range(rounds):
        own_pieces += [[piece] for piece in on_side([held[mine][turn]]) + on_side([crossed[2 * turn]])]
    step, distances = side // 2, [0]
    while step >= 1:
        distances += [distance ^ step for distance in distances]
        step //= 2
    distances += [distance ^ side for distance in distances]
    near = jnp.bitwise_xor(jnp.array(distances, dtype=jnp.int32), own)
    exchange = (near[:, None] == jnp.arange(vec_parts, dtype=jnp.int32)[None, :]).astype(jnp.float32)
    order = jnp.kron(jnp.eye(rounds, dtype=jnp.float32), jnp.kron(exchange, jnp.eye(hil_parts, dtype=jnp.float32)))
    order_own = order.reshape(rounds, vec_parts, hil_parts, -1)[:, 0].reshape(vec_local, -1)
    partial = gram_partial(own_pieces, lax.rem(own, side), side)
    partial = dot(order, dot(partial, order, (1, 0), highest), (0, 0), highest)
    partial, first, back = lax.optimization_barrier((partial, crossed[-1], held[mine][-1]))
    cuts = [back[:, :, begin:end] for begin, end in zip(bounds[1:], bounds[2:])]
    partial, cuts = lax.optimization_barrier((small_sum(partial, "vec"), cuts))
    cuts = [first] + spread_step(cuts, side)
    gram_sum, cuts[1] = lax.optimization_barrier((small_sum(partial, "hil"), cuts[1]))
    mixing = newton_schulz(gram_sum) * math.sqrt(up_count * down_count)
    mixing = dot(dot(order_own, mixing, (1, 1), highest), order, (1, 1), highest)
    wide = jnp.arange(vec_local * SUBLANES, dtype=jnp.int32)
    long = jnp.arange(order.shape[0] * SUBLANES, dtype=jnp.int32)
    left = (wide[:, None] % vec_local == jnp.arange(vec_local, dtype=jnp.int32)[None, :]).astype(jnp.float32)
    right = (jnp.arange(order.shape[0], dtype=jnp.int32)[:, None] == long[None, :] // SUBLANES).astype(jnp.float32)
    wide_mixing = dot(left, dot(mixing, right, (1, 0), highest), (1, 0), highest)
    wide_mixing = jnp.where(wide[:, None] // vec_local == long[None, :] % SUBLANES, wide_mixing, 0.0)
    wide_mixing, cuts[:3] = lax.optimization_barrier((wide_mixing, cuts[:3]))
    result = rotate_part(own_pieces, wide_mixing, place, mine, 0, down_count, None)
    result, cuts[3] = lax.optimization_barrier((result, cuts[3]))
    here = [[piece] for turn in range(rounds) for piece in on_side([held[theirs][turn]])]
    there = [[piece] for turn in range(rounds - 1) for piece in on_side([crossed[2 * turn + 1]])]
    exchanged = [on_side([cut]) for cut in cuts]
    early = there + [list(pair) for pair in zip(*exchanged[:3])]
    late = there + [[piece] for piece in exchanged[3]]
    for arrays, column, width in ((early, 0, bounds[3]), (late, 3, down_count - bounds[3])):
        pieces = []
        for begin in range(0, len(here), side):
            pieces += here[begin : begin + side] + arrays[begin : begin + side]
        result = rotate_part(pieces, wide_mixing, place, theirs, column, width, result)
    return result


def split_down(local_block):
    hil_parts = lax.axis_size("hil")
    up_local, vec_local, down_count = local_block.shape
    down_local = down_count // hil_parts
    arranged = local_block.reshape(up_local, vec_local, hil_parts, down_local).transpose(2, 0, 1, 3)
    arranged = arranged.reshape(hil_parts, up_local, vec_local * down_local)
    received = lax.all_to_all(arranged, "hil", split_axis=0, concat_axis=1, tiled=True)
    return received.reshape(hil_parts * up_local, vec_local * down_local)


def split_up(spread, up_local, vec_local):
    hil_parts = lax.axis_size("hil")
    total_up, columns = spread.shape
    down_local = columns // vec_local
    received = lax.all_to_all(
        spread.reshape(1, total_up, columns), "hil", split_axis=1, concat_axis=0, tiled=True
    )
    arranged = received.reshape(hil_parts, up_local, vec_local, down_local).transpose(1, 2, 0, 3)
    return arranged.reshape(up_local, vec_local, hil_parts * down_local)


def advance(applied, present, earlier, degree_step):
    if degree_step == 0:
        return (applied - center_shift * present) / half_range
    return 2.0 * (applied - center_shift * present) / half_range - earlier


def down_cut(start_block, down_matrix, hop_coef, hop_partner, onsite_u):
    up_local, vec_local, down_count = start_block.shape
    up_matrix = hop_matrix(hop_coef, hop_partner)
    sites = onsite_u.shape[0]
    local_states = lax.axis_index("hil") * up_local + jnp.arange(up_local, dtype=jnp.int32)
    interaction = jnp.dot(
        site_bits(local_states, sites) * onsite_u[None, :],
        site_bits(jnp.arange(down_count, dtype=jnp.int32), sites).T,
        precision=highest,
        preferred_element_type=jnp.float32,
    )
    current = previous = start_block
    current_cut = previous_cut = split_down(current)
    for degree_step in range(DEGREE):
        local_part = dot(current.reshape(up_local * vec_local, down_count), down_matrix, (1, 1), high)
        local_part = local_part.reshape(current.shape) + interaction[:, None, :] * current
        hopped = dot(up_matrix, current_cut, (1, 0), high)
        applied = local_part + split_up(hopped, up_local, vec_local)
        following = advance(applied, current, previous, degree_step)
        if degree_step + 1 < DEGREE:
            applied_cut = split_down(local_part) + hopped
            following_cut = advance(applied_cut, current_cut, previous_cut, degree_step)
            previous_cut, current_cut = current_cut, following_cut
        previous, current = current, following
    row_panel = lax.all_to_all(current, "vec", split_axis=2, concat_axis=1, tiled=True)
    gram_sum = lax.psum(jnp.einsum("ukd,uld->kl", row_panel, row_panel, precision=highest), ("hil", "vec"))
    mixing = newton_schulz(gram_sum) * math.sqrt(up_matrix.shape[0] * down_count)
    row_panel = jnp.einsum("ukd,kl->uld", row_panel, mixing, precision=highest)
    return lax.all_to_all(row_panel, "vec", split_axis=1, concat_axis=2, tiled=True)


def on_device(start_block, down_matrix, hop_partner, hop_sign, bond_hop, onsite_u):
    hil_parts, vec_parts = lax.axis_size("hil"), lax.axis_size("vec")
    up_local, vec_local, _ = start_block.shape
    hop_coef = -bond_hop[:, None] * hop_sign.astype(jnp.float32)
    whole_vectors = vec_local % hil_parts == 0 and hil_parts % 8 == 0
    halved = vec_parts > 1 and vec_parts & (vec_parts - 1) == 0 and up_local % (16 * vec_parts) == 0
    plan = vector_cut if whole_vectors and halved else down_cut
    return plan(start_block, down_matrix, hop_coef, hop_partner, onsite_u)


def solution(mesh):
    in_specs = (P("hil", "vec", None), P(), P(), P(), P(), P())
    out_specs = P("hil", "vec", None)
    return jax.shard_map(
        on_device, mesh=mesh, in_specs=in_specs, out_specs=out_specs, check_vma=False
    )
```

```python
import functools
import math

import jax
import jax.numpy as jnp
from jax import lax
from jax.experimental import pallas as pl
from jax.experimental.pallas import tpu as pltpu
from jax.sharding import PartitionSpec as P

DEGREE = 2
NS_ITERS = 4
SUBLANES = 8
STACK = 4

highest = lax.Precision.HIGHEST
high = lax.Precision.HIGH
center_shift = 6.0
half_range = 12.0


def site_bits(states, sites):
    shifts = jnp.arange(sites, dtype=jnp.int32)
    return jnp.bitwise_and(jnp.right_shift(states[:, None], shifts[None, :]), 1).astype(jnp.float32)


def hop_matrix(hop_coef, hop_partner):
    up_count = hop_partner.shape[1]
    columns = jnp.arange(up_count, dtype=jnp.int32)
    total = jnp.zeros((up_count, up_count), jnp.float32)
    for bond in range(hop_partner.shape[0]):
        total = total + jnp.where(hop_partner[bond][:, None] == columns[None, :], hop_coef[bond][:, None], 0.0)
    return total


def dot(left, right, contract, precision):
    return lax.dot_general(
        left, right, ((contract[:1], contract[1:]), ((), ())), precision=precision, preferred_element_type=jnp.float32
    )


def apply_rows(vector, vector_rows, down_matrix, up_rows, diagonal_rows):
    applied = dot(vector_rows, down_matrix, (1, 1), high) + dot(up_rows, vector, (1, 0), high)
    return applied + diagonal_rows * vector_rows


def spread_step(held, step):
    pairs = [(i, i ^ step) for i in range(lax.axis_size("vec"))]
    return [lax.ppermute(piece, "vec", pairs) for piece in held]


def split(values):
    top = values.astype(jnp.bfloat16)
    return top, (values - top.astype(jnp.float32)).astype(jnp.bfloat16)


def vectors_first_kernel(place_ref, block_ref, out_ref):
    out_ref[...] = jnp.swapaxes(block_ref[...], 0, 1)


def vectors_first(start_block, turn, count, place):
    up_local, _, down_count = start_block.shape
    rows = min(32, up_local // 2)
    blocks = up_local // rows
    return pl.pallas_call(
        vectors_first_kernel,
        out_shape=jax.ShapeDtypeStruct((count, up_local, down_count), jnp.float32),
        grid_spec=pltpu.PrefetchScalarGridSpec(
            num_scalar_prefetch=1,
            grid=(blocks,),
            in_specs=[
                pl.BlockSpec(
                    (rows, count, down_count),
                    lambda i, place: (lax.rem(i + place[0] * (blocks // 2), blocks), turn, 0),
                )
            ],
            out_specs=pl.BlockSpec((count, rows, down_count), lambda i, place: (0, i, 0)),
        ),
        compiler_params=pltpu.CompilerParams(vmem_limit_bytes=56 * 1024 * 1024),
    )(place, start_block)


def joined(refs):
    return jnp.concatenate([ref[...] for ref in refs], axis=-1)


def grouped(refs, counts):
    ends = [sum(counts[: i + 1]) for i in range(len(counts))]
    return [refs[end - count : end] for end, count in zip(ends, counts)]


def stacked(refs, counts):
    return jnp.concatenate([jnp.swapaxes(joined(cuts), 0, 1) for cuts in grouped(refs, counts)], axis=1)


def gram_kernel(counts, start_ref, *refs):
    inputs, (top_ref, cross_ref) = refs[:-2], refs[-2:]

    @pl.when(pl.program_id(0) == 0)
    def _():
        top_ref[...] = jnp.zeros_like(top_ref)
        cross_ref[...] = jnp.zeros_like(cross_ref)

    values = stacked(inputs, counts)
    rows, vectors, columns = values.shape
    for first in range(0, rows, STACK):
        top, low = split(values[first : first + STACK].reshape(STACK * vectors, columns))
        top_ref[...] += dot(top, top, (1, 1), None)
        cross_ref[...] += dot(top, low, (1, 1), None)


def gram_partial(pieces, part, parts):
    vectors = sum(cuts[0].shape[0] for cuts in pieces)
    blocks = pieces[0][0].shape[1] // parts // SUBLANES
    flat = [cut for cuts in pieces for cut in cuts]
    specs = [
        pl.BlockSpec((cut.shape[0], SUBLANES, cut.shape[2]), lambda i, first: (0, first[0] + i, 0)) for cut in flat
    ]
    size = STACK * vectors
    out = jax.ShapeDtypeStruct((size, size), jnp.float32)
    top, cross = pl.pallas_call(
        functools.partial(gram_kernel, [len(cuts) for cuts in pieces]),
        out_shape=(out, out),
        grid_spec=pltpu.PrefetchScalarGridSpec(
            num_scalar_prefetch=1,
            grid=(blocks,),
            in_specs=specs,
            out_specs=[pl.BlockSpec((size, size), lambda i, first: (0, 0))] * 2,
        ),
        compiler_params=pltpu.CompilerParams(vmem_limit_bytes=48 * 1024 * 1024),
        cost_estimate=pl.CostEstimate(
            flops=4 * size * size * flat[0].shape[2] * blocks * SUBLANES // STACK,
            bytes_accessed=4 * sum(cut.size for cut in flat) // parts,
            transcendentals=0,
        ),
    )((part * blocks).reshape(1), *flat)
    cross = cross + cross.T
    total = (top + cross).reshape(STACK, vectors, STACK, vectors)
    return sum(total[u, :, u, :] for u in range(STACK))


def rotate_kernel(counts, place_ref, mix_ref, *refs):
    inputs, out_ref, both_ref = refs[: sum(counts)], refs[-2], refs[-1]
    rows, _, columns = out_ref.shape
    count = mix_ref.shape[0]

    @pl.when(pl.program_id(0) == 0)
    def _():
        mix_top, mix_low = split(mix_ref[...])
        both_ref[:count] = mix_top
        both_ref[count:] = mix_low

    for first in range(0, rows, SUBLANES):
        blocks = []
        for cuts in grouped(inputs, counts):
            block = jnp.concatenate([ref[:, first : first + SUBLANES, :] for ref in cuts], axis=-1)
            blocks.append(block.reshape(-1, columns))
        top, low = split(jnp.concatenate(blocks, axis=0))
        wide = dot(both_ref[...], top, (1, 0), None)
        result = wide[:count] + wide[count:] + dot(both_ref[:count], low, (1, 0), None)
        out_ref[first : first + SUBLANES] = result.reshape(SUBLANES, -1, columns)


def rotate_part(pieces, wide_mixing, place, half, column, width, earlier):
    half_rows = pieces[0][0].shape[1]
    down_count = pieces[0][0].shape[2]
    step_rows = 2 * SUBLANES
    blocks = half_rows // step_rows
    own = wide_mixing.shape[0] // SUBLANES
    flat = [cut for cuts in pieces for cut in cuts]
    specs = [pl.BlockSpec(wide_mixing.shape, lambda i, place: (0, 0))]
    for cut in flat:
        shape = (cut.shape[0], step_rows, min(cut.shape[2], width))
        specs.append(pl.BlockSpec(shape, lambda i, place, at=column if cut.shape[2] == down_count else 0: (0, i, at)))
    operands = [place, wide_mixing, *flat]
    aliases = {}
    if earlier is not None:
        specs.append(pl.BlockSpec(memory_space=pl.ANY))
        aliases = {len(operands): 0}
        operands.append(earlier)
    return pl.pallas_call(
        functools.partial(rotate_kernel, [len(cuts) for cuts in pieces]),
        out_shape=jax.ShapeDtypeStruct((2 * half_rows, own, down_count), jnp.float32),
        grid_spec=pltpu.PrefetchScalarGridSpec(
            num_scalar_prefetch=1,
            grid=(blocks,),
            in_specs=specs,
            out_specs=pl.BlockSpec(
                (step_rows, own, width), lambda i, place: (i + lax.rem(place[0] + half, 2) * blocks, 0, column)
            ),
            scratch_shapes=[pltpu.VMEM((2 * wide_mixing.shape[0], wide_mixing.shape[1]), jnp.bfloat16)],
        ),
        input_output_aliases=aliases,
        compiler_params=pltpu.CompilerParams(vmem_limit_bytes=56 * 1024 * 1024),
        cost_estimate=pl.CostEstimate(flops=0, bytes_accessed=0, transcendentals=0),
    )(*operands)


def small_sum(values, axis):
    parts = lax.axis_size(axis)
    if parts & (parts - 1):
        return lax.psum(values, axis)
    step = 1
    while step < parts:
        count = min(4, parts // step)
        moved = []
        for distance in range(step, count * step, step):
            moved.append(lax.ppermute(values, axis, [(i, i ^ distance) for i in range(parts)]))
        for other in moved:
            values = values + other
        step *= count
    return values


def newton_schulz(gram_sum):
    identity = jnp.eye(gram_sum.shape[0], dtype=jnp.float32)
    norm_scale = 1.0 / jnp.sqrt(jnp.sqrt(jnp.sum(gram_sum * gram_sum)) + 1e-06)
    gram_sum = norm_scale * norm_scale * gram_sum
    product_total = identity
    for _ in range(NS_ITERS):
        mixing = 1.5 * identity - 0.5 * gram_sum
        product_total = dot(product_total, mixing, (1, 0), highest)
        gram_sum = dot(mixing, dot(gram_sum, mixing, (1, 0), highest), (1, 0), highest)
    return norm_scale * product_total


def vector_cut(start_block, down_matrix, hop_coef, hop_partner, onsite_u):
    hil_parts, vec_parts = lax.axis_size("hil"), lax.axis_size("vec")
    up_local, vec_local, down_count = start_block.shape
    up_count = up_local * hil_parts
    rounds = vec_local // hil_parts
    half_rows = up_local // 2
    side = vec_parts // 2
    own = lax.axis_index("vec")
    swap = own // side
    place = swap.reshape(1).astype(jnp.int32)

    def ordered(values):
        cut = values.reshape(values.shape[:-1] + (hil_parts, 2, half_rows))
        return jnp.where(swap == 1, cut[..., ::-1, :], cut).reshape(values.shape)

    arrived = []
    for turn in range(rounds):
        block = vectors_first(start_block, turn, hil_parts, place)
        block = lax.all_to_all(block, "hil", split_axis=0, concat_axis=0, tiled=True)
        arrived.append(block.reshape(up_count, down_count))
    other = jnp.where((hop_partner // half_rows) % 2 == 0, hop_partner + half_rows, hop_partner - half_rows)
    up_matrix = hop_matrix(ordered(hop_coef), ordered(jnp.where(swap == 1, other, hop_partner)))
    sites = onsite_u.shape[0]
    diagonal = -center_shift + jnp.dot(
        site_bits(ordered(jnp.arange(up_count, dtype=jnp.int32)), sites) * onsite_u[None, :],
        site_bits(jnp.arange(down_count, dtype=jnp.int32), sites).T,
        precision=highest,
        preferred_element_type=jnp.float32,
    )

    def rows(values, half):
        return values.reshape(hil_parts, 2, half_rows, -1)[:, half].reshape(hil_parts * half_rows, -1)

    def first_step(vector):
        return apply_rows(vector, vector, down_matrix, up_matrix, diagonal) / half_range

    def second_step(vector, before, half):
        applied = apply_rows(vector, rows(vector, half), down_matrix, rows(up_matrix, half), rows(diagonal, half))
        return (2.0 * applied / half_range - rows(before, half)).reshape(hil_parts, half_rows, down_count)

    mine, theirs = 0, 1
    once = first_step(arrived[0])
    pieces = [second_step(once, arrived[0], half) for half in (mine, theirs)]
    pieces[theirs], pieces[mine] = lax.optimization_barrier((pieces[theirs], pieces[mine]))
    crossed = []
    held = [[], []]
    for turn in range(rounds):
        upcoming = [None, None]
        for half in (theirs, mine):
            piece = pieces[half]
            if half == mine and turn + 1 < rounds:
                once = first_step(arrived[turn + 1])
                upcoming[theirs] = second_step(once, arrived[turn + 1], theirs)
                piece, once, upcoming[theirs] = lax.optimization_barrier((piece, once, upcoming[theirs]))
                upcoming[mine] = second_step(once, arrived[turn + 1], mine)
            if len(crossed) > 1:
                piece, crossed[-2] = lax.optimization_barrier((piece, crossed[-2]))
            back = lax.all_to_all(piece, "hil", split_axis=0, concat_axis=0, tiled=True)
            held[half].append(back)
            if (turn, half) == (rounds - 1, mine):
                bounds = [down_count // 4 * number for number in range(5)]
                crossed.append(spread_step([back[:, :, : bounds[1]]], side)[0])
            else:
                crossed.append(spread_step([back], side)[0])
        pieces = upcoming

    def on_side(near):
        step = side // 2
        while step >= 1:
            near = near + spread_step(near, step)
            step //= 2
        return near

    own_pieces = []
    for turn in range(rounds):
        own_pieces += [[piece] for piece in on_side([held[mine][turn]]) + on_side([crossed[2 * turn]])]
    step, distances = side // 2, [0]
    while step >= 1:
        distances += [distance ^ step for distance in distances]
        step //= 2
    distances += [distance ^ side for distance in distances]
    near = jnp.bitwise_xor(jnp.array(distances, dtype=jnp.int32), own)
    exchange = (near[:, None] == jnp.arange(vec_parts, dtype=jnp.int32)[None, :]).astype(jnp.float32)
    order = jnp.kron(jnp.eye(rounds, dtype=jnp.float32), jnp.kron(exchange, jnp.eye(hil_parts, dtype=jnp.float32)))
    order_own = order.reshape(rounds, vec_parts, hil_parts, -1)[:, 0].reshape(vec_local, -1)
    partial = gram_partial(own_pieces, lax.rem(own, side), side)
    partial = dot(order, dot(partial, order, (1, 0), highest), (0, 0), highest)
    partial, first, back = lax.optimization_barrier((partial, crossed[-1], held[mine][-1]))
    cuts = [back[:, :, begin:end] for begin, end in zip(bounds[1:], bounds[2:])]
    partial, cuts = lax.optimization_barrier((small_sum(partial, "vec"), cuts))
    cuts = [first] + spread_step(cuts, side)
    gram_sum, cuts[1] = lax.optimization_barrier((small_sum(partial, "hil"), cuts[1]))
    mixing = newton_schulz(gram_sum) * math.sqrt(up_count * down_count)
    mixing = dot(dot(order_own, mixing, (1, 1), highest), order, (1, 1), highest)
    wide = jnp.arange(vec_local * SUBLANES, dtype=jnp.int32)
    long = jnp.arange(order.shape[0] * SUBLANES, dtype=jnp.int32)
    left = (wide[:, None] % vec_local == jnp.arange(vec_local, dtype=jnp.int32)[None, :]).astype(jnp.float32)
    right = (jnp.arange(order.shape[0], dtype=jnp.int32)[:, None] == long[None, :] // SUBLANES).astype(jnp.float32)
    wide_mixing = dot(left, dot(mixing, right, (1, 0), highest), (1, 0), highest)
    wide_mixing = jnp.where(wide[:, None] // vec_local == long[None, :] % SUBLANES, wide_mixing, 0.0)
    here = [[piece] for turn in range(rounds) for piece in on_side([held[theirs][turn]])]
    there = [[piece] for turn in range(rounds - 1) for piece in on_side([crossed[2 * turn + 1]])]
    exchanged = [on_side([cut]) for cut in cuts[:2]]
    wide_mixing, here, there, exchanged = lax.optimization_barrier((wide_mixing, here, there, exchanged))
    result = rotate_part(own_pieces, wide_mixing, place, mine, 0, down_count, None)
    for column in range(2):
        result, cuts[2 + column] = lax.optimization_barrier((result, cuts[2 + column]))
        exchanged.append(on_side([cuts[2 + column]]))
        arrays = there + [list(pair) for pair in zip(*exchanged[2 * column : 2 * column + 2])]
        pieces = []
        for begin in range(0, len(here), side):
            pieces += here[begin : begin + side] + arrays[begin : begin + side]
        result = rotate_part(pieces, wide_mixing, place, theirs, column, down_count // 2, result)
    return result


def split_down(local_block):
    hil_parts = lax.axis_size("hil")
    up_local, vec_local, down_count = local_block.shape
    down_local = down_count // hil_parts
    arranged = local_block.reshape(up_local, vec_local, hil_parts, down_local).transpose(2, 0, 1, 3)
    arranged = arranged.reshape(hil_parts, up_local, vec_local * down_local)
    received = lax.all_to_all(arranged, "hil", split_axis=0, concat_axis=1, tiled=True)
    return received.reshape(hil_parts * up_local, vec_local * down_local)


def split_up(spread, up_local, vec_local):
    hil_parts = lax.axis_size("hil")
    total_up, columns = spread.shape
    down_local = columns // vec_local
    received = lax.all_to_all(
        spread.reshape(1, total_up, columns), "hil", split_axis=1, concat_axis=0, tiled=True
    )
    arranged = received.reshape(hil_parts, up_local, vec_local, down_local).transpose(1, 2, 0, 3)
    return arranged.reshape(up_local, vec_local, hil_parts * down_local)


def advance(applied, present, earlier, degree_step):
    if degree_step == 0:
        return (applied - center_shift * present) / half_range
    return 2.0 * (applied - center_shift * present) / half_range - earlier


def down_cut(start_block, down_matrix, hop_coef, hop_partner, onsite_u):
    up_local, vec_local, down_count = start_block.shape
    up_matrix = hop_matrix(hop_coef, hop_partner)
    sites = onsite_u.shape[0]
    local_states = lax.axis_index("hil") * up_local + jnp.arange(up_local, dtype=jnp.int32)
    interaction = jnp.dot(
        site_bits(local_states, sites) * onsite_u[None, :],
        site_bits(jnp.arange(down_count, dtype=jnp.int32), sites).T,
        precision=highest,
        preferred_element_type=jnp.float32,
    )
    current = previous = start_block
    current_cut = previous_cut = split_down(current)
    for degree_step in range(DEGREE):
        local_part = dot(current.reshape(up_local * vec_local, down_count), down_matrix, (1, 1), high)
        local_part = local_part.reshape(current.shape) + interaction[:, None, :] * current
        hopped = dot(up_matrix, current_cut, (1, 0), high)
        applied = local_part + split_up(hopped, up_local, vec_local)
        following = advance(applied, current, previous, degree_step)
        if degree_step + 1 < DEGREE:
            applied_cut = split_down(local_part) + hopped
            following_cut = advance(applied_cut, current_cut, previous_cut, degree_step)
            previous_cut, current_cut = current_cut, following_cut
        previous, current = current, following
    row_panel = lax.all_to_all(current, "vec", split_axis=2, concat_axis=1, tiled=True)
    gram_sum = lax.psum(jnp.einsum("ukd,uld->kl", row_panel, row_panel, precision=highest), ("hil", "vec"))
    mixing = newton_schulz(gram_sum) * math.sqrt(up_matrix.shape[0] * down_count)
    row_panel = jnp.einsum("ukd,kl->uld", row_panel, mixing, precision=highest)
    return lax.all_to_all(row_panel, "vec", split_axis=1, concat_axis=2, tiled=True)


def on_device(start_block, down_matrix, hop_partner, hop_sign, bond_hop, onsite_u):
    hil_parts, vec_parts = lax.axis_size("hil"), lax.axis_size("vec")
    up_local, vec_local, _ = start_block.shape
    hop_coef = -bond_hop[:, None] * hop_sign.astype(jnp.float32)
    whole_vectors = vec_local % hil_parts == 0 and hil_parts % 8 == 0
    halved = vec_parts > 1 and vec_parts & (vec_parts - 1) == 0 and up_local % (16 * vec_parts) == 0
    plan = vector_cut if whole_vectors and halved else down_cut
    return plan(start_block, down_matrix, hop_coef, hop_partner, onsite_u)


def solution(mesh):
    in_specs = (P("hil", "vec", None), P(), P(), P(), P(), P())
    out_specs = P("hil", "vec", None)
    return jax.shard_map(
        on_device, mesh=mesh, in_specs=in_specs, out_specs=out_specs, check_vma=False
    )
```

```python
import functools
import math

import jax
import jax.numpy as jnp
from jax import lax
from jax.experimental import pallas as pl
from jax.experimental.pallas import tpu as pltpu
from jax.sharding import PartitionSpec as P

DEGREE = 2
NS_ITERS = 4
SUBLANES = 8
STACK = 4

highest = lax.Precision.HIGHEST
high = lax.Precision.HIGH
center_shift = 6.0
half_range = 12.0


def site_bits(states, sites):
    shifts = jnp.arange(sites, dtype=jnp.int32)
    return jnp.bitwise_and(jnp.right_shift(states[:, None], shifts[None, :]), 1).astype(jnp.float32)


def hop_matrix(hop_coef, hop_partner):
    up_count = hop_partner.shape[1]
    columns = jnp.arange(up_count, dtype=jnp.int32)
    total = jnp.zeros((up_count, up_count), jnp.float32)
    for bond in range(hop_partner.shape[0]):
        total = total + jnp.where(hop_partner[bond][:, None] == columns[None, :], hop_coef[bond][:, None], 0.0)
    return total


def dot(left, right, contract, precision):
    return lax.dot_general(
        left, right, ((contract[:1], contract[1:]), ((), ())), precision=precision, preferred_element_type=jnp.float32
    )


def apply_rows(vector, vector_rows, down_matrix, up_rows, diagonal_rows):
    applied = dot(vector_rows, down_matrix, (1, 1), high) + dot(up_rows, vector, (1, 0), high)
    return applied + diagonal_rows * vector_rows


def spread_step(held, step):
    pairs = [(i, i ^ step) for i in range(lax.axis_size("vec"))]
    return [lax.ppermute(piece, "vec", pairs) for piece in held]


def split(values):
    top = values.astype(jnp.bfloat16)
    return top, (values - top.astype(jnp.float32)).astype(jnp.bfloat16)


def vectors_first_kernel(place_ref, block_ref, out_ref):
    out_ref[...] = jnp.swapaxes(block_ref[...], 0, 1)


def vectors_first(start_block, turn, count, place):
    up_local, _, down_count = start_block.shape
    rows = min(32, up_local // 2)
    blocks = up_local // rows
    return pl.pallas_call(
        vectors_first_kernel,
        out_shape=jax.ShapeDtypeStruct((count, up_local, down_count), jnp.float32),
        grid_spec=pltpu.PrefetchScalarGridSpec(
            num_scalar_prefetch=1,
            grid=(blocks,),
            in_specs=[
                pl.BlockSpec(
                    (rows, count, down_count),
                    lambda i, place: (lax.rem(i + place[0] * (blocks // 2), blocks), turn, 0),
                )
            ],
            out_specs=pl.BlockSpec((count, rows, down_count), lambda i, place: (0, i, 0)),
        ),
        compiler_params=pltpu.CompilerParams(vmem_limit_bytes=56 * 1024 * 1024),
    )(place, start_block)


def joined(refs):
    return jnp.concatenate([ref[...] for ref in refs], axis=-1)


def grouped(refs, counts):
    ends = [sum(counts[: i + 1]) for i in range(len(counts))]
    return [refs[end - count : end] for end, count in zip(ends, counts)]


def stacked(refs, counts):
    return jnp.concatenate([jnp.swapaxes(joined(cuts), 0, 1) for cuts in grouped(refs, counts)], axis=1)


def gram_kernel(counts, start_ref, *refs):
    inputs, (top_ref, cross_ref) = refs[:-2], refs[-2:]

    @pl.when(pl.program_id(0) == 0)
    def _():
        top_ref[...] = jnp.zeros_like(top_ref)
        cross_ref[...] = jnp.zeros_like(cross_ref)

    values = stacked(inputs, counts)
    rows, vectors, columns = values.shape
    for first in range(0, rows, STACK):
        top, low = split(values[first : first + STACK].reshape(STACK * vectors, columns))
        top_ref[...] += dot(top, top, (1, 1), None)
        cross_ref[...] += dot(top, low, (1, 1), None)


def gram_partial(pieces, part, parts):
    vectors = sum(cuts[0].shape[0] for cuts in pieces)
    blocks = pieces[0][0].shape[1] // parts // SUBLANES
    flat = [cut for cuts in pieces for cut in cuts]
    specs = [
        pl.BlockSpec((cut.shape[0], SUBLANES, cut.shape[2]), lambda i, first: (0, first[0] + i, 0)) for cut in flat
    ]
    size = STACK * vectors
    out = jax.ShapeDtypeStruct((size, size), jnp.float32)
    top, cross = pl.pallas_call(
        functools.partial(gram_kernel, [len(cuts) for cuts in pieces]),
        out_shape=(out, out),
        grid_spec=pltpu.PrefetchScalarGridSpec(
            num_scalar_prefetch=1,
            grid=(blocks,),
            in_specs=specs,
            out_specs=[pl.BlockSpec((size, size), lambda i, first: (0, 0))] * 2,
        ),
        compiler_params=pltpu.CompilerParams(vmem_limit_bytes=48 * 1024 * 1024),
        cost_estimate=pl.CostEstimate(
            flops=4 * size * size * flat[0].shape[2] * blocks * SUBLANES // STACK,
            bytes_accessed=4 * sum(cut.size for cut in flat) // parts,
            transcendentals=0,
        ),
    )((part * blocks).reshape(1), *flat)
    cross = cross + cross.T
    total = (top + cross).reshape(STACK, vectors, STACK, vectors)
    return sum(total[u, :, u, :] for u in range(STACK))


def rotate_kernel(counts, place_ref, mix_ref, *refs):
    inputs, out_ref, both_ref = refs[: sum(counts)], refs[-2], refs[-1]
    rows, _, columns = out_ref.shape
    count = mix_ref.shape[0]

    @pl.when(pl.program_id(0) == 0)
    def _():
        mix_top, mix_low = split(mix_ref[...])
        both_ref[:count] = mix_top
        both_ref[count:] = mix_low

    for first in range(0, rows, SUBLANES):
        blocks = []
        for cuts in grouped(inputs, counts):
            block = jnp.concatenate([ref[:, first : first + SUBLANES, :] for ref in cuts], axis=-1)
            blocks.append(block.reshape(-1, columns))
        top, low = split(jnp.concatenate(blocks, axis=0))
        wide = dot(both_ref[...], top, (1, 0), None)
        result = wide[:count] + wide[count:] + dot(both_ref[:count], low, (1, 0), None)
        out_ref[first : first + SUBLANES] = result.reshape(SUBLANES, -1, columns)


def rotate_part(pieces, wide_mixing, place, half, column, width, earlier):
    half_rows = pieces[0][0].shape[1]
    down_count = pieces[0][0].shape[2]
    step_rows = 2 * SUBLANES
    blocks = half_rows // step_rows
    own = wide_mixing.shape[0] // SUBLANES
    flat = [cut for cuts in pieces for cut in cuts]
    specs = [pl.BlockSpec(wide_mixing.shape, lambda i, place: (0, 0))]
    for cut in flat:
        shape = (cut.shape[0], step_rows, min(cut.shape[2], width))
        specs.append(pl.BlockSpec(shape, lambda i, place, at=column if cut.shape[2] == down_count else 0: (0, i, at)))
    operands = [place, wide_mixing, *flat]
    aliases = {}
    if earlier is not None:
        specs.append(pl.BlockSpec(memory_space=pl.ANY))
        aliases = {len(operands): 0}
        operands.append(earlier)
    return pl.pallas_call(
        functools.partial(rotate_kernel, [len(cuts) for cuts in pieces]),
        out_shape=jax.ShapeDtypeStruct((2 * half_rows, own, down_count), jnp.float32),
        grid_spec=pltpu.PrefetchScalarGridSpec(
            num_scalar_prefetch=1,
            grid=(blocks,),
            in_specs=specs,
            out_specs=pl.BlockSpec(
                (step_rows, own, width), lambda i, place: (i + lax.rem(place[0] + half, 2) * blocks, 0, column)
            ),
            scratch_shapes=[pltpu.VMEM((2 * wide_mixing.shape[0], wide_mixing.shape[1]), jnp.bfloat16)],
        ),
        input_output_aliases=aliases,
        compiler_params=pltpu.CompilerParams(vmem_limit_bytes=30 * 1024 * 1024),
        cost_estimate=pl.CostEstimate(flops=0, bytes_accessed=0, transcendentals=0),
    )(*operands)


def small_sum(values, axis):
    parts = lax.axis_size(axis)
    if parts & (parts - 1):
        return lax.psum(values, axis)
    step = 1
    while step < parts:
        count = min(4, parts // step)
        moved = []
        for distance in range(step, count * step, step):
            moved.append(lax.ppermute(values, axis, [(i, i ^ distance) for i in range(parts)]))
        for other in moved:
            values = values + other
        step *= count
    return values


def newton_schulz(gram_sum):
    identity = jnp.eye(gram_sum.shape[0], dtype=jnp.float32)
    norm_scale = 1.0 / jnp.sqrt(jnp.sqrt(jnp.sum(gram_sum * gram_sum)) + 1e-06)
    gram_sum = norm_scale * norm_scale * gram_sum
    product_total = identity
    for _ in range(NS_ITERS):
        mixing = 1.5 * identity - 0.5 * gram_sum
        product_total = dot(product_total, mixing, (1, 0), highest)
        gram_sum = dot(mixing, dot(gram_sum, mixing, (1, 0), highest), (1, 0), highest)
    return norm_scale * product_total


def vector_cut(start_block, down_matrix, hop_coef, hop_partner, onsite_u):
    hil_parts, vec_parts = lax.axis_size("hil"), lax.axis_size("vec")
    up_local, vec_local, down_count = start_block.shape
    up_count = up_local * hil_parts
    rounds = vec_local // hil_parts
    half_rows = up_local // 2
    side = vec_parts // 2
    own = lax.axis_index("vec")
    swap = own // side
    place = swap.reshape(1).astype(jnp.int32)

    def ordered(values):
        cut = values.reshape(values.shape[:-1] + (hil_parts, 2, half_rows))
        return jnp.where(swap == 1, cut[..., ::-1, :], cut).reshape(values.shape)

    arrived = []
    for turn in range(rounds):
        block = vectors_first(start_block, turn, hil_parts, place)
        block = lax.all_to_all(block, "hil", split_axis=0, concat_axis=0, tiled=True)
        arrived.append(block.reshape(up_count, down_count))
    other = jnp.where((hop_partner // half_rows) % 2 == 0, hop_partner + half_rows, hop_partner - half_rows)
    up_matrix = hop_matrix(ordered(hop_coef), ordered(jnp.where(swap == 1, other, hop_partner)))
    sites = onsite_u.shape[0]
    diagonal = -center_shift + jnp.dot(
        site_bits(ordered(jnp.arange(up_count, dtype=jnp.int32)), sites) * onsite_u[None, :],
        site_bits(jnp.arange(down_count, dtype=jnp.int32), sites).T,
        precision=highest,
        preferred_element_type=jnp.float32,
    )

    def rows(values, half):
        return values.reshape(hil_parts, 2, half_rows, -1)[:, half].reshape(hil_parts * half_rows, -1)

    def first_step(vector):
        return apply_rows(vector, vector, down_matrix, up_matrix, diagonal) / half_range

    def second_step(vector, before, half):
        applied = apply_rows(vector, rows(vector, half), down_matrix, rows(up_matrix, half), rows(diagonal, half))
        return (2.0 * applied / half_range - rows(before, half)).reshape(hil_parts, half_rows, down_count)

    mine, theirs = 0, 1
    once = first_step(arrived[0])
    pieces = [second_step(once, arrived[0], half) for half in (mine, theirs)]
    pieces[theirs], pieces[mine] = lax.optimization_barrier((pieces[theirs], pieces[mine]))
    crossed = []
    held = [[], []]
    for turn in range(rounds):
        upcoming = [None, None]
        for half in (theirs, mine):
            piece = pieces[half]
            if half == mine and turn + 1 < rounds:
                once = first_step(arrived[turn + 1])
                upcoming[theirs] = second_step(once, arrived[turn + 1], theirs)
                piece, once, upcoming[theirs] = lax.optimization_barrier((piece, once, upcoming[theirs]))
                upcoming[mine] = second_step(once, arrived[turn + 1], mine)
            if len(crossed) > 1:
                piece, crossed[-2] = lax.optimization_barrier((piece, crossed[-2]))
            back = lax.all_to_all(piece, "hil", split_axis=0, concat_axis=0, tiled=True)
            held[half].append(back)
            if (turn, half) == (rounds - 1, mine):
                bounds = [down_count // 4 * number for number in range(5)]
                crossed.append(spread_step([back[:, :, : bounds[1]]], side)[0])
            else:
                crossed.append(spread_step([back], side)[0])
        pieces = upcoming

    def on_side(near):
        step = side // 2
        while step >= 1:
            near = near + spread_step(near, step)
            step //= 2
        return near

    own_pieces = []
    for turn in range(rounds):
        own_pieces += [[piece] for piece in on_side([held[mine][turn]]) + on_side([crossed[2 * turn]])]
    step, distances = side // 2, [0]
    while step >= 1:
        distances += [distance ^ step for distance in distances]
        step //= 2
    distances += [distance ^ side for distance in distances]
    near = jnp.bitwise_xor(jnp.array(distances, dtype=jnp.int32), own)
    exchange = (near[:, None] == jnp.arange(vec_parts, dtype=jnp.int32)[None, :]).astype(jnp.float32)
    order = jnp.kron(jnp.eye(rounds, dtype=jnp.float32), jnp.kron(exchange, jnp.eye(hil_parts, dtype=jnp.float32)))
    order_own = order.reshape(rounds, vec_parts, hil_parts, -1)[:, 0].reshape(vec_local, -1)
    partial = gram_partial(own_pieces, lax.rem(own, side), side)
    partial = dot(order, dot(partial, order, (1, 0), highest), (0, 0), highest)
    partial, first, back = lax.optimization_barrier((partial, crossed[-1], held[mine][-1]))
    cuts = [back[:, :, begin:end] for begin, end in zip(bounds[1:], bounds[2:])]
    partial, cuts = lax.optimization_barrier((small_sum(partial, "vec"), cuts))
    cuts = [first] + spread_step(cuts, side)
    gram_sum, cuts[1] = lax.optimization_barrier((small_sum(partial, "hil"), cuts[1]))
    mixing = newton_schulz(gram_sum) * math.sqrt(up_count * down_count)
    mixing = dot(dot(order_own, mixing, (1, 1), highest), order, (1, 1), highest)
    wide = jnp.arange(vec_local * SUBLANES, dtype=jnp.int32)
    long = jnp.arange(order.shape[0] * SUBLANES, dtype=jnp.int32)
    left = (wide[:, None] % vec_local == jnp.arange(vec_local, dtype=jnp.int32)[None, :]).astype(jnp.float32)
    right = (jnp.arange(order.shape[0], dtype=jnp.int32)[:, None] == long[None, :] // SUBLANES).astype(jnp.float32)
    wide_mixing = dot(left, dot(mixing, right, (1, 0), highest), (1, 0), highest)
    wide_mixing = jnp.where(wide[:, None] // vec_local == long[None, :] % SUBLANES, wide_mixing, 0.0)
    here = [[piece] for turn in range(rounds) for piece in on_side([held[theirs][turn]])]
    there = [[piece] for turn in range(rounds - 1) for piece in on_side([crossed[2 * turn + 1]])]
    exchanged = [on_side([cut]) for cut in cuts[:2]]
    wide_mixing, here, there, exchanged = lax.optimization_barrier((wide_mixing, here, there, exchanged))
    result = rotate_part(own_pieces, wide_mixing, place, mine, 0, down_count, None)
    for column in range(2):
        result, cuts[2 + column] = lax.optimization_barrier((result, cuts[2 + column]))
        exchanged.append(on_side([cuts[2 + column]]))
        arrays = there + [list(pair) for pair in zip(*exchanged[2 * column : 2 * column + 2])]
        pieces = []
        for begin in range(0, len(here), side):
            pieces += here[begin : begin + side] + arrays[begin : begin + side]
        result = rotate_part(pieces, wide_mixing, place, theirs, column, down_count // 2, result)
    return result


def split_down(local_block):
    hil_parts = lax.axis_size("hil")
    up_local, vec_local, down_count = local_block.shape
    down_local = down_count // hil_parts
    arranged = local_block.reshape(up_local, vec_local, hil_parts, down_local).transpose(2, 0, 1, 3)
    arranged = arranged.reshape(hil_parts, up_local, vec_local * down_local)
    received = lax.all_to_all(arranged, "hil", split_axis=0, concat_axis=1, tiled=True)
    return received.reshape(hil_parts * up_local, vec_local * down_local)


def split_up(spread, up_local, vec_local):
    hil_parts = lax.axis_size("hil")
    total_up, columns = spread.shape
    down_local = columns // vec_local
    received = lax.all_to_all(
        spread.reshape(1, total_up, columns), "hil", split_axis=1, concat_axis=0, tiled=True
    )
    arranged = received.reshape(hil_parts, up_local, vec_local, down_local).transpose(1, 2, 0, 3)
    return arranged.reshape(up_local, vec_local, hil_parts * down_local)


def advance(applied, present, earlier, degree_step):
    if degree_step == 0:
        return (applied - center_shift * present) / half_range
    return 2.0 * (applied - center_shift * present) / half_range - earlier


def down_cut(start_block, down_matrix, hop_coef, hop_partner, onsite_u):
    up_local, vec_local, down_count = start_block.shape
    up_matrix = hop_matrix(hop_coef, hop_partner)
    sites = onsite_u.shape[0]
    local_states = lax.axis_index("hil") * up_local + jnp.arange(up_local, dtype=jnp.int32)
    interaction = jnp.dot(
        site_bits(local_states, sites) * onsite_u[None, :],
        site_bits(jnp.arange(down_count, dtype=jnp.int32), sites).T,
        precision=highest,
        preferred_element_type=jnp.float32,
    )
    current = previous = start_block
    current_cut = previous_cut = split_down(current)
    for degree_step in range(DEGREE):
        local_part = dot(current.reshape(up_local * vec_local, down_count), down_matrix, (1, 1), high)
        local_part = local_part.reshape(current.shape) + interaction[:, None, :] * current
        hopped = dot(up_matrix, current_cut, (1, 0), high)
        applied = local_part + split_up(hopped, up_local, vec_local)
        following = advance(applied, current, previous, degree_step)
        if degree_step + 1 < DEGREE:
            applied_cut = split_down(local_part) + hopped
            following_cut = advance(applied_cut, current_cut, previous_cut, degree_step)
            previous_cut, current_cut = current_cut, following_cut
        previous, current = current, following
    row_panel = lax.all_to_all(current, "vec", split_axis=2, concat_axis=1, tiled=True)
    gram_sum = lax.psum(jnp.einsum("ukd,uld->kl", row_panel, row_panel, precision=highest), ("hil", "vec"))
    mixing = newton_schulz(gram_sum) * math.sqrt(up_matrix.shape[0] * down_count)
    row_panel = jnp.einsum("ukd,kl->uld", row_panel, mixing, precision=highest)
    return lax.all_to_all(row_panel, "vec", split_axis=1, concat_axis=2, tiled=True)


def on_device(start_block, down_matrix, hop_partner, hop_sign, bond_hop, onsite_u):
    hil_parts, vec_parts = lax.axis_size("hil"), lax.axis_size("vec")
    up_local, vec_local, _ = start_block.shape
    hop_coef = -bond_hop[:, None] * hop_sign.astype(jnp.float32)
    whole_vectors = vec_local % hil_parts == 0 and hil_parts % 8 == 0
    halved = vec_parts > 1 and vec_parts & (vec_parts - 1) == 0 and up_local % (16 * vec_parts) == 0
    plan = vector_cut if whole_vectors and halved else down_cut
    return plan(start_block, down_matrix, hop_coef, hop_partner, onsite_u)


def solution(mesh):
    in_specs = (P("hil", "vec", None), P(), P(), P(), P(), P())
    out_specs = P("hil", "vec", None)
    return jax.shard_map(
        on_device, mesh=mesh, in_specs=in_specs, out_specs=out_specs, check_vma=False
    )
```
